512 devices in a mesh: energy: 128 (over y, x, z_lo, core), elem: 4 (over z_hi).
Axes of the slice: x: 4, y: 4, z: 16 (z_hi: 4, z_lo: 4; z = z_hi * 4 + z_lo), core: 2. Of those that a mesh axis runs over, the one named last changes fastest.
Arguments:
- lesser_green: float32 [2, 4096, 2048], P(None, 'energy', 'elem'), may hold values from -6 to 6
- greater_green: float32 [2, 4096, 2048], P(None, 'energy', 'elem'), may hold values from -6 to 6
- partner: int32 [2048], P('elem'), may hold values from 0 to 2047, as said below
Outputs:
- lesser_polar: float32 [2, 4096, 2048], P(None, 'energy', 'elem')
- greater_polar: float32 [2, 4096, 2048], P(None, 'energy', 'elem')
The draws below stay inside these ranges and needn't reach their ends.
Inputs may be any that keep to these rules, and one draw needn't show every extreme that they name: partner is an involution without fixed points: partner[partner[e]] = e and partner[e] != e; pairs may join elements of different groups.
All inputs are finite; a program needn't handle non-finite values.
Results may differ from the reference program's by a relative error of at most 0.000098.
Values sent between devices are 32-bit elements; how exact they have to be, the bound alone decides.
A program may use at most 64 MiB of HBM per device.

```python
import jax
import jax.numpy as jnp
from jax import lax

NE = 4096
ELOC = 4
ELEMS = 2048


def draw_partner(key, part):
    key = jax.random.fold_in(key, 7)
    shuffled = jax.random.permutation(key, ELEMS).astype(jnp.int32)
    swapped = shuffled.reshape(-1, 2)[:, ::-1].reshape(-1)
    return jnp.zeros((ELEMS,), jnp.int32).at[shuffled].set(swapped)


def level_of(stream_key, extent, pieces, low, high):
    level, own = 1.0, jax.random.fold_in(stream_key, 6)
    for position, blocks in pieces:
        heights = jnp.exp(jax.random.uniform(jax.random.fold_in(own, position), (blocks,), jnp.float32, low / len(pieces), high / len(pieces)))
        level = level * jnp.repeat(heights, extent[position] // blocks).reshape([-1 if axis == position else 1 for axis in range(len(extent))])
    return level


def bell_draw(rng, shape, scale, bound, cuts=(), held_as=jnp.bfloat16):
    values = jax.random.normal(rng, shape, jnp.float32) * scale
    if len(cuts) > 0:
        values = level_of(rng, shape, cuts, -0.22, 0.18) * values
    return jnp.clip(values, min=-bound, max=bound).astype(held_as)


def setup_inputs(seed: int = 0) -> dict:
    seeds = jax.random.split(jax.random.key(seed), 4)
    return {
        "lesser_green": bell_draw(seeds[0], (2, NE, ELEMS), 1.0, 6.0, ((1, 128), (2, 4)), jnp.float32),
        "greater_green": bell_draw(seeds[1], (2, NE, ELEMS), 1.0, 6.0, ((1, 128), (2, 4)), jnp.float32),
        "partner": draw_partner(jax.random.fold_in(seeds[3], 71), 0),
    }


def lag_product(first_real, first_imag, second_real, second_imag):
    energies = first_real.shape[1]
    first = jnp.fft.fft(lax.complex(first_real, first_imag), n=2 * energies, axis=1)
    second = jnp.fft.fft(lax.complex(second_real, second_imag)[:, ::-1], n=2 * energies, axis=1)
    convolved = jnp.fft.ifft(first * second, axis=1)[:, energies - 1:2 * energies - 1]
    scale = energies ** -0.5
    return jnp.stack([-scale * jnp.imag(convolved).T, scale * jnp.real(convolved).T])


def reference(lesser_green, greater_green, partner):
    greater_swapped = jnp.take(greater_green, partner, axis=2)
    lesser_swapped = jnp.take(lesser_green, partner, axis=2)

    def stack_blocks(field):
        return field.reshape(2, NE, ELEMS // ELOC, ELOC).transpose(2, 0, 1, 3)

    def one_block(fields):
        first, second, third, fourth = fields
        lesser_part = lag_product(first[0].T, first[1].T, second[0].T, second[1].T)
        greater_part = lag_product(third[0].T, third[1].T, fourth[0].T, fourth[1].T)
        return lesser_part, greater_part

    lesser_blocks, greater_blocks = lax.map(one_block, (stack_blocks(lesser_green), stack_blocks(greater_swapped), stack_blocks(greater_green), stack_blocks(lesser_swapped)))

    def unstack(blocks):
        return blocks.transpose(1, 2, 0, 3).reshape(2, NE, ELEMS)

    return unstack(lesser_blocks), unstack(greater_blocks)
```

```python
import jax
import jax.numpy as jnp
import numpy as np
from jax import lax
from jax.experimental import pallas as pl
from jax.experimental.pallas import tpu as pltpu
from jax.sharding import PartitionSpec as P

PLANE, DEPTH, GROUPS, MLOC = 32, 4, 4, 32
LINE = DEPTH * GROUPS
ROWS, LANES = 256, 128
PERIOD = 8192
MESH = pl.DeviceIdType.MESH


def split(table):
    high = table.astype(jnp.bfloat16)
    low = (table - high.astype(np.float32)).astype(jnp.bfloat16)
    return high, low


def tables():
    row = np.arange(ROWS)
    plane, zl, part = row // 8, row // 2 % 4, row % 2
    index = plane // 2 * 8 + zl * 2 + plane % 2
    freq = np.arange(ROWS)
    angle = 2 * np.pi * (freq[:, None] * index[None, :] % ROWS) / ROWS
    cos, sin = np.cos(angle), np.sin(angle)
    first = np.concatenate(
        [np.where(part == 0, cos, sin), np.where(part == 0, -sin, cos)], 0
    )
    scale = 1.0 / (64 * PERIOD)
    last = scale * np.concatenate(
        [np.where(part == 0, sin, cos).T, np.where(part == 0, -cos, sin).T], 1
    )
    lane = np.arange(LANES)
    local, el = lane % MLOC, lane // MLOC
    same = (el[:, None] == el[None, :]).astype(np.float64)
    angle = 2 * np.pi * (local[:, None] * local[None, :] % MLOC) / MLOC
    cos, sin = same * np.cos(angle), same * np.sin(angle)
    middle = np.block([[cos, -sin], [sin, cos]])
    angle = 2 * np.pi * (freq[:, None] * local[None, :]) / PERIOD
    turn = np.stack([np.cos(angle), np.sin(angle)]).astype(np.float32)
    out = []
    for table in (first, middle, last):
        out.extend(split(table.astype(np.float32)))
    return [*out, turn]


def parts_of(x):
    high = x.astype(jnp.bfloat16)
    return high, (x - high.astype(jnp.float32)).astype(jnp.bfloat16)


def mm(a, b):
    return jnp.dot(a, b, preferred_element_type=jnp.float32)


def table_times(high, low, x):
    xh, xl = parts_of(x)
    return mm(high, xh) + (mm(high, xl) + mm(low, xh))


def times_table(x, high, low):
    xh, xl = parts_of(x)
    return mm(xh, high) + (mm(xl, high) + mm(xh, low))


def odd_rows(shape):
    return lax.broadcasted_iota(jnp.int32, shape, 0) % 2 == 1


def turned(real, imag, cos, sin):
    return real * cos + imag * sin, imag * cos - real * sin


def both(left, right):
    return jnp.concatenate([left, right], axis=1)


def correlate(a, b, f1h, f1l, f2h, f2l, gh, gl, turn):
    odd = odd_rows((ROWS, LANES))
    x = both(a, jnp.where(odd, -b, b))
    cos, sin = both(turn[0], turn[0]), both(turn[1], turn[1])
    y = table_times(f1h, f1l, x)
    yr, yi = turned(y[:ROWS], y[ROWS:], cos, sin)
    z = times_table(
        jnp.concatenate(
            [both(yr[:, :LANES], yi[:, :LANES]), both(yr[:, LANES:], yi[:, LANES:])], 0
        ),
        f2h,
        f2l,
    )
    ar, ai = z[:ROWS, :LANES], z[:ROWS, LANES:]
    br, bi = z[ROWS:, :LANES], z[ROWS:, LANES:]
    cr, ci = ar * br + ai * bi, ai * br - ar * bi
    v = times_table(jnp.concatenate([both(cr, ci), both(cr, -ci)], 0), f2h, f2l)
    er, ei = turned(
        both(v[:ROWS, :LANES], v[ROWS:, :LANES]),
        both(v[:ROWS, LANES:], v[ROWS:, LANES:]),
        cos,
        sin,
    )
    out = table_times(gh, gl, jnp.concatenate([er, ei], 0))
    q, p = out[:, :LANES], out[:, LANES:]
    return q, jnp.where(odd, p, -p)


def blocks_swapped(t):
    cut = [[t[32 * i : 32 * i + 32, 32 * j : 32 * j + 32] for j in range(4)] for i in range(4)]
    return [jnp.concatenate([cut[i][j] for i in range(4)], axis=1) for j in range(4)]


def to_owner(block, out):
    for part in range(2):
        t = jnp.concatenate([block(zl, part) for zl in range(4)], 0).T
        for zl, rows in enumerate(blocks_swapped(t)):
            out[:, zl * 2 + part, :] = rows


def to_energies(got, store):
    for part in range(2):
        rows = jnp.concatenate([got[:, zl * 2 + part, :] for zl in range(4)], 0)
        t = jnp.concatenate(blocks_swapped(rows), 0).T
        for zl in range(4):
            store(zl, part, t[32 * zl : 32 * zl + 32])


def permute(src, dst, order):
    def tile(d, carry):
        at = jnp.broadcast_to(order[d], (8, LANES))
        lane, where = at % LANES, at // LANES
        for part in range(2):
            total = jnp.zeros((8, LANES), jnp.float32)
            for s in range(LINE):
                piece = src[part, :, s * LANES : (s + 1) * LANES]
                moved = jnp.take_along_axis(piece, lane, axis=1)
                total = jnp.where(where == s, moved, total)
            dst[part, :, pl.ds(pl.multiple_of(d * LANES, LANES), LANES)] = total
        return carry

    lax.fori_loop(0, LINE, tile, 0)


def kernel(
    lesser, greater, partner, f1h, f1l, f2h, f2l, gh, gl, turn,
    lesser_out, greater_out,
    order, z1, swapped, z2, zl_in, send_a, send_b, own_a, own_b,
    back_q, back_p, got_q, got_p, wide_q, wide_p, z2_back, unswapped,
    sems, line_send, plane_send, few_send, local_sem,
):
    energy, zh = lax.axis_index("energy"), lax.axis_index("elem")
    w, zl = energy // 8 * 2 + energy % 2, energy // 2 % DEPTH
    z = zh * DEPTH + zl

    def device(plane, low, high):
        return {"energy": plane // 2 * 8 + low * 2 + plane % 2, "elem": high}

    def line_peer(i):
        step = i // 2 + 1
        other = (z + LINE + step * (1 - 2 * (i % 2))) % LINE
        return other % DEPTH, other // DEPTH

    def plane_peer(i):
        return (w + 1 + i) % PLANE

    barrier = pltpu.get_barrier_semaphore()

    def greet_line(i, c):
        low, high = line_peer(i)
        pl.semaphore_signal(barrier, inc=1, device_id=device(w, low, high), device_id_type=MESH)
        return c

    def greet_plane(i, c):
        pl.semaphore_signal(
            barrier, inc=1, device_id=device(plane_peer(i), zl, zh), device_id_type=MESH
        )
        return c

    lax.fori_loop(0, LINE - 1, greet_line, 0)
    lax.fori_loop(0, PLANE - 1, greet_plane, 0)
    pl.semaphore_wait(barrier, LINE - 1 + PLANE - 1)

    def remote(src, dst, send, recv, where):
        return pltpu.make_async_remote_copy(
            src_ref=src, dst_ref=dst, send_sem=send, recv_sem=recv,
            device_id=where, device_id_type=MESH,
        )

    def arrived(whole, sem):
        pltpu.make_async_copy(whole, whole, sem).wait()

    def quarter(ref, h):
        return ref.at[:, pl.ds(pl.multiple_of(h * 8, 8), 8), :]

    def lanes(ref, start, size):
        return ref.at[:, :, pl.ds(pl.multiple_of(start, LANES), size)]

    def groups(phase, src, dst, recv):
        copies = []
        for i in range(GROUPS - 1):
            h = (zh + 1 + i) % GROUPS
            copies.append(remote(src(h), dst, few_send.at[phase, i], recv, device(w, zl, h)))
        for copy in copies:
            copy.start()
        mine = pltpu.make_async_copy(src(zh), dst, recv)
        mine.start()
        return copies

    def depths(phase, src, dst, recv):
        copies = []
        for i in range(DEPTH - 1):
            low = (zl + 1 + i) % DEPTH
            copies.append(remote(src(low), dst, few_send.at[phase, i], recv, device(w, low, zh)))
        for copy in copies:
            copy.start()
        mine = pltpu.make_async_copy(src(zl), dst, recv)
        mine.start()
        return copies

    def line_copy(phase, src, dst, recv, i):
        low, high = line_peer(i)
        return remote(src(low, high), dst, line_send.at[phase, i], recv, device(w, low, high))

    def line(phase, src, dst, recv):
        def start(i, c):
            line_copy(phase, src, dst, recv, i).start()
            return c

        lax.fori_loop(0, LINE - 1, start, 0)
        pltpu.make_async_copy(src(zl, zh), dst, recv).start()

    def line_done(phase, src, dst, recv):
        def done(i, c):
            line_copy(phase, src, dst, recv, i).wait_send()
            return c

        lax.fori_loop(0, LINE - 1, done, 0)

    def plane_copy(phase, src, dst, recv, i):
        other = plane_peer(i)
        return remote(
            src.at[other], dst.at[w], plane_send.at[phase, i], recv, device(other, zl, zh)
        )

    def plane(phase, src, dst, recv):
        def start(i, c):
            plane_copy(phase, src, dst, recv, i).start()
            return c

        lax.fori_loop(0, PLANE - 1, start, 0)
        pltpu.make_async_copy(src.at[w], dst.at[w], recv).start()

    def plane_done(phase, src, dst, recv):
        def done(i, c):
            plane_copy(phase, src, dst, recv, i).wait_send()
            return c

        lax.fori_loop(0, PLANE - 1, done, 0)

    started = []
    started += groups(0, lambda h: partner, order.at[zh], sems.at[0])
    started += groups(1, lambda h: quarter(greater, h), lanes(z1, zh * 512, 512), sems.at[1])
    started += depths(2, lambda low: lanes(lesser, low * LANES, LANES), zl_in.at[zl], sems.at[2])
    arrived(zl_in, sems.at[2])
    to_owner(lambda low, part: zl_in[low, part], send_a)
    plane(0, send_a, own_a, sems.at[3])
    arrived(order, sems.at[0])
    arrived(z1, sems.at[1])
    flat = order.reshape(LINE, 1, LANES)
    permute(z1, swapped, flat)

    def swapped_src(low, high):
        return lanes(swapped, (high * DEPTH + low) * LANES, LANES)

    z2_dst = z2.at[zl, :, zh]
    line(0, swapped_src, z2_dst, sems.at[4])
    arrived(z2, sems.at[4])
    to_owner(lambda low, part: z2[low, part].reshape(MLOC, LANES), send_b)
    plane(1, send_b, own_b, sems.at[5])
    arrived(own_a, sems.at[3])
    arrived(own_b, sems.at[5])
    q, p = correlate(
        own_a[...].reshape(ROWS, LANES), own_b[...].reshape(ROWS, LANES),
        f1h[...], f1l[...], f2h[...], f2l[...], gh[...], gl[...], turn[...],
    )
    back_q[...] = q.reshape(PLANE, 8, LANES)
    plane(2, back_q, got_q, sems.at[6])
    back_p[...] = p.reshape(PLANE, 8, LANES)
    plane(3, back_p, got_p, sems.at[7])
    arrived(got_q, sems.at[6])

    def keep_q(low, part, rows):
        wide_q[low, part] = rows.reshape(GROUPS, 8, LANES)

    to_energies(got_q, keep_q)

    def wide_src(low, high):
        return wide_q.at[low, :, high]

    back_dst = lanes(z2_back, z * LANES, LANES)
    line(1, wide_src, back_dst, sems.at[8])
    arrived(got_p, sems.at[7])

    def keep_p(low, part, rows):
        wide_p[low, part] = rows

    to_energies(got_p, keep_p)
    started += depths(3, lambda low: wide_p.at[low], lanes(lesser_out, zl * LANES, LANES), sems.at[9])
    arrived(z2_back, sems.at[8])
    permute(z2_back, unswapped, flat)
    started += groups(4, lambda h: lanes(unswapped, h * 512, 512), quarter(greater_out, zh), sems.at[10])
    arrived(lesser_out, sems.at[9])
    arrived(greater_out, sems.at[10])
    for copy in started:
        copy.wait_send()
    line_done(0, swapped_src, z2_dst, sems.at[4])
    line_done(1, wide_src, back_dst, sems.at[8])
    plane_done(0, send_a, own_a, sems.at[3])
    plane_done(1, send_b, own_b, sems.at[5])
    plane_done(2, back_q, got_q, sems.at[6])
    plane_done(3, back_p, got_p, sems.at[7])


def per_device(lesser, greater, partner):
    f32 = jnp.float32
    field = jax.ShapeDtypeStruct((2, MLOC, 512), f32)
    owned = pltpu.VMEM((PLANE, 8, LANES), f32)
    long = pltpu.VMEM((2, 8, 2048), f32)
    deep = pltpu.VMEM((DEPTH, 2, MLOC, LANES), f32)
    cut = pltpu.VMEM((DEPTH, 2, GROUPS, 8, LANES), f32)
    vmem = pl.BlockSpec(memory_space=pltpu.VMEM)
    constants = [jnp.asarray(table) for table in tables()]
    return pl.pallas_call(
        kernel,
        out_shape=(field, field),
        in_specs=[vmem] * 10,
        out_specs=(vmem, vmem),
        scratch_shapes=[
            pltpu.VMEM((GROUPS, 4, 1, LANES), jnp.int32),
            long, long, cut, deep, owned, owned, owned, owned,
            owned, owned, owned, owned, cut, deep, long, long,
            pltpu.SemaphoreType.DMA((11,)),
            pltpu.SemaphoreType.DMA((2, LINE - 1)),
            pltpu.SemaphoreType.DMA((4, PLANE - 1)),
            pltpu.SemaphoreType.DMA((5, 3)),
            pltpu.SemaphoreType.DMA,
        ],
        compiler_params=pltpu.CompilerParams(
            collective_id=0, has_side_effects=True, vmem_limit_bytes=48 * 1024 * 1024
        ),
    )(lesser, greater, partner.reshape(4, 1, LANES), *constants)


def solution(mesh):
    placed = (P(None, "energy", "elem"), P(None, "energy", "elem"), P("elem"))
    return jax.shard_map(
        per_device,
        mesh=mesh,
        in_specs=placed,
        out_specs=(P(None, "energy", "elem"), P(None, "energy", "elem")),
        check_vma=False,
    )
```

```python
import jax
import jax.numpy as jnp
import numpy as np
from jax import lax
from jax.experimental import pallas as pl
from jax.experimental.pallas import tpu as pltpu
from jax.sharding import PartitionSpec as P

PLANE, DEPTH, GROUPS, MLOC = 32, 4, 4, 32
LINE = DEPTH * GROUPS
ROWS, LANES = 256, 128
PERIOD = 8192
MESH = pl.DeviceIdType.MESH


def split(table):
    high = table.astype(jnp.bfloat16)
    low = (table - high.astype(np.float32)).astype(jnp.bfloat16)
    return high, low


def tables():
    row = np.arange(ROWS)
    part, zl, plane = row // LANES, row // PLANE % DEPTH, row % PLANE
    index = plane // 2 * 8 + zl * 2 + plane % 2
    freq = np.arange(ROWS)
    angle = 2 * np.pi * (freq[:, None] * index[None, :] % ROWS) / ROWS
    cos, sin = np.cos(angle), np.sin(angle)
    first = np.concatenate(
        [np.where(part == 0, cos, sin), np.where(part == 0, -sin, cos)], 0
    )
    scale = 1.0 / (64 * PERIOD)
    last = scale * np.concatenate(
        [np.where(part == 0, sin, cos).T, np.where(part == 0, -cos, sin).T], 1
    )
    lane = np.arange(LANES)
    local, el = lane % MLOC, lane // MLOC
    same = (el[:, None] == el[None, :]).astype(np.float64)
    angle = 2 * np.pi * (local[:, None] * local[None, :] % MLOC) / MLOC
    cos, sin = same * np.cos(angle), same * np.sin(angle)
    middle = np.block([[cos, -sin], [sin, cos]])
    angle = 2 * np.pi * (freq[:, None] * local[None, :]) / PERIOD
    turn = np.stack([np.cos(angle), np.sin(angle)]).astype(np.float32)
    out = []
    for table in (first, middle, last):
        out.extend(split(table.astype(np.float32)))
    return [*out, turn]


def parts_of(x):
    high = x.astype(jnp.bfloat16)
    return high, (x - high.astype(jnp.float32)).astype(jnp.bfloat16)


def mm(a, b):
    return jnp.dot(a, b, preferred_element_type=jnp.float32)


def table_times(high, low, x):
    xh, xl = parts_of(x)
    return mm(high, xh) + (mm(high, xl) + mm(low, xh))


def times_table(x, high, low):
    xh, xl = parts_of(x)
    return mm(xh, high) + (mm(xl, high) + mm(xh, low))


def turned(real, imag, cos, sin):
    return real * cos + imag * sin, imag * cos - real * sin


def both(left, right):
    return jnp.concatenate([left, right], axis=1)


def correlate(a, b, f1h, f1l, f2h, f2l, gh, gl, turn):
    x = both(a, jnp.concatenate([b[:LANES], -b[LANES:]], 0))
    cos, sin = both(turn[0], turn[0]), both(turn[1], turn[1])
    y = table_times(f1h, f1l, x)
    yr, yi = turned(y[:ROWS], y[ROWS:], cos, sin)
    z = times_table(
        jnp.concatenate(
            [both(yr[:, :LANES], yi[:, :LANES]), both(yr[:, LANES:], yi[:, LANES:])], 0
        ),
        f2h,
        f2l,
    )
    ar, ai = z[:ROWS, :LANES], z[:ROWS, LANES:]
    br, bi = z[ROWS:, :LANES], z[ROWS:, LANES:]
    cr, ci = ar * br + ai * bi, ai * br - ar * bi
    v = times_table(jnp.concatenate([both(cr, ci), both(cr, -ci)], 0), f2h, f2l)
    er, ei = turned(
        both(v[:ROWS, :LANES], v[ROWS:, :LANES]),
        both(v[:ROWS, LANES:], v[ROWS:, LANES:]),
        cos,
        sin,
    )
    out = table_times(gh, gl, jnp.concatenate([er, ei], 0))
    q, p = out[:, :LANES], out[:, LANES:]
    return q, jnp.concatenate([-p[:LANES], p[LANES:]], 0)


def blocks_swapped(t):
    cut = [[t[32 * i : 32 * i + 32, 32 * j : 32 * j + 32] for j in range(4)] for i in range(4)]
    return [jnp.concatenate([cut[i][j] for i in range(4)], axis=1) for j in range(4)]


def to_owner(block, out):
    t = jnp.concatenate([block(zl) for zl in range(DEPTH)], 0).T
    for zl, rows in enumerate(blocks_swapped(t)):
        out[:, zl, :] = rows


def to_energies(got, store):
    rows = jnp.concatenate([got[:, zl, :] for zl in range(DEPTH)], 0)
    t = jnp.concatenate(blocks_swapped(rows), 0).T
    for zl in range(DEPTH):
        store(zl, t[MLOC * zl : MLOC * zl + MLOC])


def permute(src, dst, order):
    def tile(d, carry):
        at = jnp.broadcast_to(order[d], (8, LANES))
        lane, where = at % LANES, at // LANES
        total = jnp.zeros((8, LANES), jnp.float32)
        for s in range(LINE):
            moved = jnp.take_along_axis(src[:, s * LANES : (s + 1) * LANES], lane, axis=1)
            total = jnp.where(where == s, moved, total)
        dst[:, pl.ds(pl.multiple_of(d * LANES, LANES), LANES)] = total
        return carry

    lax.fori_loop(0, LINE, tile, 0)


def kernel(
    lesser, greater, partner, *refs,
):
    tables_in, refs = refs[:7], refs[7:]
    lesser_out, greater_out = refs[:2]
    tables_here, refs = refs[2:9], refs[9:]
    (
        order, z1, swapped, z2, zl_in, send_a, send_b, own_a, own_b,
        back_q, back_p, got_q, got_p, wide_q, wide_p, z2_back, unswapped,
        table_sem, sems, line_send, plane_send, few_send,
    ) = refs
    energy, zh = lax.axis_index("energy"), lax.axis_index("elem")
    w, zl = energy // 8 * 2 + energy % 2, energy // 2 % DEPTH
    z = zh * DEPTH + zl
    parts = (0, 1)

    def device(plane, low, high):
        return {"energy": plane // 2 * 8 + low * 2 + plane % 2, "elem": high}

    def line_peer(i):
        other = (z + LINE + (LINE // 2 - (i + 1) // 2) * (1 - 2 * (i % 2))) % LINE
        return other % DEPTH, other // DEPTH

    def far(t):
        return (54 >> (2 * t)) % 4

    def plane_peer(i):
        y = (w // 8 + far(i // 8)) % 4
        x = (w // 2 + far(i // 2 % 4)) % 4
        return y * 8 + x * 2 + (w + 1 + i) % 2

    def meet_zl(low):
        return (low + 2) % DEPTH

    def meet_zh(low, h):
        return (h + (low + 2) // DEPTH) % GROUPS

    def met_quarter(low, high):
        return (high + GROUPS - (3 - low) // 2) % GROUPS

    barrier = pltpu.get_barrier_semaphore()

    def greet_line(i, c):
        low, high = line_peer(i)
        pl.semaphore_signal(barrier, inc=1, device_id=device(w, low, high), device_id_type=MESH)
        return c

    def greet_plane(i, c):
        pl.semaphore_signal(
            barrier, inc=1, device_id=device(plane_peer(i), zl, zh), device_id_type=MESH
        )
        return c

    lax.fori_loop(0, LINE - 1, greet_line, 0)
    lax.fori_loop(0, PLANE - 1, greet_plane, 0)
    table_copies = [
        pltpu.make_async_copy(src, dst, table_sem.at[i])
        for i, (src, dst) in enumerate(zip(tables_in, tables_here))
    ]
    for copy in table_copies:
        copy.start()
    pl.semaphore_wait(barrier, LINE - 1 + PLANE - 1)

    def remote(src, dst, send, recv, where):
        return pltpu.make_async_remote_copy(
            src_ref=src, dst_ref=dst, send_sem=send, recv_sem=recv,
            device_id=where, device_id_type=MESH,
        )

    def arrived(whole, sem):
        pltpu.make_async_copy(whole, whole, sem).wait()

    def quarter(ref, part, h):
        return ref.at[part, pl.ds(pl.multiple_of(h * 8, 8), 8), :]

    def lanes(ref, start, size):
        return ref.at[..., pl.ds(pl.multiple_of(start, LANES), size)]

    started = []

    def send(phase, i, src, dst, recv, where):
        copy = remote(src, dst, few_send.at[phase, i], recv, where)
        copy.start()
        started.append(copy)

    def meet(phase, src, dst, recv):
        for i in range(GROUPS):
            h = (zh + 1 + i) % GROUPS
            send(phase, i, src(h), dst, recv, device(w, meet_zl(zl), meet_zh(zl, h)))

    def leave(phase, src, dst, recv):
        for i in range(GROUPS):
            h = (zh + 1 + i) % GROUPS
            send(phase, i, src(h), dst, recv, device(w, meet_zl(zl), h))

    def depths(phase, src, dst, recv):
        for i in range(DEPTH - 1):
            low = (zl + 1 + i) % DEPTH
            send(phase, i, src(low), dst, recv, device(w, low, zh))
        pltpu.make_async_copy(src(zl), dst, recv).start()

    def line_copy(phase, src, dst, recv, i):
        low, high = line_peer(i)
        return remote(src(low, high), dst, line_send.at[phase, i], recv, device(w, low, high))

    def line(phase, src, dst, recv):
        def start(i, c):
            line_copy(phase, src, dst, recv, i).start()
            return c

        lax.fori_loop(0, LINE - 1, start, 0)
        pltpu.make_async_copy(src(zl, zh), dst, recv).start()

    def line_done(phase, src, dst, recv):
        def done(i, c):
            line_copy(phase, src, dst, recv, i).wait_send()
            return c

        lax.fori_loop(0, LINE - 1, done, 0)

    def plane_copy(phase, src, dst, recv, i):
        other = plane_peer(i)
        return remote(
            src(other), dst(w), plane_send.at[phase, i], recv, device(other, zl, zh)
        )

    def plane(phase, src, dst, recv):
        def start(i, c):
            plane_copy(phase, src, dst, recv, i).start()
            return c

        lax.fori_loop(0, PLANE - 1, start, 0)
        pltpu.make_async_copy(src(w), dst(w), recv).start()

    def plane_done(phase, src, dst, recv):
        def done(i, c):
            plane_copy(phase, src, dst, recv, i).wait_send()
            return c

        lax.fori_loop(0, PLANE - 1, done, 0)

    def both_parts(ref):
        return lambda other: ref.at[:, other]

    def one_part(ref, part):
        return lambda other: ref.at[part, other]

    for i in range(GROUPS):
        h = (zh + 1 + i) % GROUPS
        send(0, i, partner, order.at[zh], sems.at[0], device(w, meet_zl(zl), h))
    for part in parts:
        meet(1 + part, lambda h: quarter(greater, part, h), lanes(z1.at[part], zh * 512, 512), sems.at[1 + part])
    depths(3, lambda low: lanes(lesser, low * LANES, LANES), zl_in.at[zl], sems.at[3])
    arrived(order, sems.at[0])
    flat = order.reshape(LINE, 1, LANES)

    def swapped_src(part):
        return lambda low, high: lanes(swapped.at[part], (high * DEPTH + low) * LANES, LANES)

    def z2_dst(part):
        return z2.at[part, meet_zl(zl), met_quarter(zl, zh)]

    for part in parts:
        arrived(z1.at[part], sems.at[1 + part])
        permute(z1.at[part], swapped.at[part], flat)
        line(part, swapped_src(part), z2_dst(part), sems.at[4 + part])
    arrived(zl_in, sems.at[3])
    for part in parts:
        to_owner(lambda low: zl_in[low, part], send_a.at[part])
    plane(0, both_parts(send_a), both_parts(own_a), sems.at[6])
    for part in parts:
        arrived(z2.at[part], sems.at[4 + part])
        to_owner(lambda low: z2[part, low].reshape(MLOC, LANES), send_b.at[part])
        plane(1 + part, one_part(send_b, part), one_part(own_b, part), sems.at[7 + part])
    arrived(own_a, sems.at[6])
    for part in parts:
        arrived(own_b.at[part], sems.at[7 + part])
    for copy in table_copies:
        copy.wait()

    def rows_of(ref):
        return jnp.concatenate([ref[part, :, low, :] for part in parts for low in range(DEPTH)], 0)

    def keep(ref, part, value):
        for low in range(DEPTH):
            ref[part, :, low, :] = value[part * LANES + low * PLANE : part * LANES + (low + 1) * PLANE]

    q, p = correlate(rows_of(own_a), rows_of(own_b), *[table[...] for table in tables_here])
    for part in parts:
        keep(back_q, part, q)
        plane(3 + part, one_part(back_q, part), one_part(got_q, part), sems.at[9 + part])
    for part in parts:
        keep(back_p, part, p)
    plane(5, both_parts(back_p), both_parts(got_p), sems.at[11])

    def wide_src(part):
        return lambda low, high: wide_q.at[part, meet_zl(low), met_quarter(low, high)]

    def back_dst(part):
        return lanes(z2_back.at[part], z * LANES, LANES)

    for part in parts:
        arrived(got_q.at[part], sems.at[9 + part])

        def keep_q(low, rows):
            wide_q[part, low] = rows.reshape(GROUPS, 8, LANES)

        to_energies(got_q.at[part], keep_q)
        line(2 + part, wide_src(part), back_dst(part), sems.at[12 + part])
    arrived(got_p, sems.at[11])
    for part in parts:

        def keep_p(low, rows):
            wide_p[low, part] = rows

        to_energies(got_p.at[part], keep_p)
    depths(4, lambda low: wide_p.at[low], lanes(lesser_out, zl * LANES, LANES), sems.at[14])
    for part in parts:
        arrived(z2_back.at[part], sems.at[12 + part])
        permute(z2_back.at[part], unswapped.at[part], flat)
        leave(
            5 + part,
            lambda h: lanes(unswapped.at[part], h * 512, 512),
            quarter(greater_out, part, met_quarter(zl, zh)),
            sems.at[15 + part],
        )
    arrived(lesser_out, sems.at[14])
    for part in parts:
        arrived(greater_out.at[part], sems.at[15 + part])
    for copy in started:
        copy.wait_send()
    plane_done(0, both_parts(send_a), both_parts(own_a), sems.at[6])
    plane_done(5, both_parts(back_p), both_parts(got_p), sems.at[11])
    for part in parts:
        line_done(part, swapped_src(part), z2_dst(part), sems.at[4 + part])
        line_done(2 + part, wide_src(part), back_dst(part), sems.at[12 + part])
        plane_done(1 + part, one_part(send_b, part), one_part(own_b, part), sems.at[7 + part])
        plane_done(3 + part, one_part(back_q, part), one_part(got_q, part), sems.at[9 + part])


def per_device(lesser, greater, partner):
    f32 = jnp.float32
    field = jax.ShapeDtypeStruct((2, MLOC, 512), f32)
    owned = pltpu.VMEM((2, PLANE, DEPTH, LANES), f32)
    long = pltpu.VMEM((2, 8, 2048), f32)
    deep = pltpu.VMEM((DEPTH, 2, MLOC, LANES), f32)
    cut = pltpu.VMEM((2, DEPTH, GROUPS, 8, LANES), f32)
    anywhere = pl.BlockSpec(memory_space=pl.ANY)
    constants = [jnp.asarray(table) for table in tables()]
    return pl.pallas_call(
        kernel,
        out_shape=(field, field),
        in_specs=[anywhere] * 10,
        out_specs=(anywhere, anywhere),
        scratch_shapes=[
            *[pltpu.VMEM(table.shape, table.dtype) for table in constants],
            pltpu.VMEM((GROUPS, 4, 1, LANES), jnp.int32),
            long, long, cut, deep, owned, owned, owned, owned,
            owned, owned, owned, owned, cut, deep, long, long,
            pltpu.SemaphoreType.DMA((7,)),
            pltpu.SemaphoreType.DMA((17,)),
            pltpu.SemaphoreType.DMA((4, LINE - 1)),
            pltpu.SemaphoreType.DMA((6, PLANE - 1)),
            pltpu.SemaphoreType.DMA((7, 4)),
        ],
        compiler_params=pltpu.CompilerParams(
            collective_id=0, has_side_effects=True, vmem_limit_bytes=48 * 1024 * 1024
        ),
    )(lesser, greater, partner.reshape(4, 1, LANES), *constants)


def solution(mesh):
    placed = (P(None, "energy", "elem"), P(None, "energy", "elem"), P("elem"))
    return jax.shard_map(
        per_device,
        mesh=mesh,
        in_specs=placed,
        out_specs=(P(None, "energy", "elem"), P(None, "energy", "elem")),
        check_vma=False,
    )
```

```python
import jax
import jax.numpy as jnp
import numpy as np
from jax import lax
from jax.experimental import pallas as pl
from jax.experimental.pallas import tpu as pltpu
from jax.sharding import PartitionSpec as P

PLANE, DEPTH, GROUPS, MLOC = 32, 4, 4, 32
LINE = DEPTH * GROUPS
ROWS, LANES = 256, 128
PERIOD = 8192
MESH = pl.DeviceIdType.MESH


def tables():
    row = np.arange(ROWS)
    part, zl, plane = row // LANES, row // PLANE % DEPTH, row % PLANE
    index = plane // 2 * 8 + zl * 2 + plane % 2
    freq = np.arange(ROWS)
    angle = 2 * np.pi * (freq[:, None] * index[None, :] % ROWS) / ROWS
    cos, sin = np.cos(angle), np.sin(angle)
    first = np.concatenate(
        [np.where(part == 0, cos, sin), np.where(part == 0, -sin, cos)], 0
    )
    scale = 1.0 / (64 * PERIOD)
    last = scale * np.concatenate(
        [np.where(part == 0, sin, cos).T, np.where(part == 0, -cos, sin).T], 1
    )
    lane = np.arange(LANES)
    local, el = lane % MLOC, lane // MLOC
    same = (el[:, None] == el[None, :]).astype(np.float64)
    angle = 2 * np.pi * (local[:, None] * local[None, :] % MLOC) / MLOC
    cos, sin = same * np.cos(angle), same * np.sin(angle)
    middle = np.block([[cos, -sin], [sin, cos]])
    angle = 2 * np.pi * (freq[:, None] * local[None, :]) / PERIOD
    turn = np.stack([np.cos(angle), np.sin(angle)]).astype(np.float32)
    return [*(table.astype(np.float32) for table in (first, middle, last)), turn]


def parts_of(x):
    high = x.astype(jnp.bfloat16)
    return high, (x - high.astype(jnp.float32)).astype(jnp.bfloat16)


def mm(a, b):
    return jnp.dot(a, b, preferred_element_type=jnp.float32)


def table_times(table, x):
    high, low = table
    xh, xl = parts_of(x)
    return mm(high, xh) + (mm(high, xl) + mm(low, xh))


def times_table(x, table):
    high, low = table
    xh, xl = parts_of(x)
    return mm(xh, high) + (mm(xl, high) + mm(xh, low))


def turned(real, imag, cos, sin):
    return real * cos + imag * sin, imag * cos - real * sin


def both(left, right):
    return jnp.concatenate([left, right], axis=1)


def correlate(a, b, first, middle, last, turn):
    x = both(a, jnp.concatenate([b[:LANES], -b[LANES:]], 0))
    cos, sin = both(turn[0], turn[0]), both(turn[1], turn[1])
    y = table_times(first, x)
    yr, yi = turned(y[:ROWS], y[ROWS:], cos, sin)
    z = times_table(
        jnp.concatenate(
            [both(yr[:, :LANES], yi[:, :LANES]), both(yr[:, LANES:], yi[:, LANES:])], 0
        ),
        middle,
    )
    ar, ai = z[:ROWS, :LANES], z[:ROWS, LANES:]
    br, bi = z[ROWS:, :LANES], z[ROWS:, LANES:]
    cr, ci = ar * br + ai * bi, ai * br - ar * bi
    v = times_table(jnp.concatenate([both(cr, ci), both(cr, -ci)], 0), middle)
    er, ei = turned(
        both(v[:ROWS, :LANES], v[ROWS:, :LANES]),
        both(v[:ROWS, LANES:], v[ROWS:, LANES:]),
        cos,
        sin,
    )
    out = table_times(last, jnp.concatenate([er, ei], 0))
    q, p = out[:, :LANES], out[:, LANES:]
    return q, jnp.concatenate([-p[:LANES], p[LANES:]], 0)


def blocks_swapped(t):
    cut = [[t[32 * i : 32 * i + 32, 32 * j : 32 * j + 32] for j in range(4)] for i in range(4)]
    return [jnp.concatenate([cut[i][j] for i in range(4)], axis=1) for j in range(4)]


def to_owner(block, out):
    t = jnp.concatenate([block(zl) for zl in range(DEPTH)], 0).T
    for zl, rows in enumerate(blocks_swapped(t)):
        out[:, zl, :] = rows


def to_energies(got, store):
    rows = jnp.concatenate([got[:, zl, :] for zl in range(DEPTH)], 0)
    t = jnp.concatenate(blocks_swapped(rows), 0).T
    for zl in range(DEPTH):
        store(zl, t[MLOC * zl : MLOC * zl + MLOC])


def permute(src, dst, order):
    def tile(d, carry):
        at = jnp.broadcast_to(order[d], (8, LANES))
        lane, where = at % LANES, at // LANES
        total = jnp.zeros((8, LANES), jnp.float32)
        for s in range(LINE):
            moved = jnp.take_along_axis(src[:, s * LANES : (s + 1) * LANES], lane, axis=1)
            total = jnp.where(where == s, moved, total)
        dst[:, pl.ds(pl.multiple_of(d * LANES, LANES), LANES)] = total
        return carry

    lax.fori_loop(0, LINE, tile, 0)


def kernel(
    lesser, greater, partner, *refs,
):
    tables_in, refs = refs[:4], refs[4:]
    lesser_out, greater_out = refs[:2]
    tables_here, halves, refs = refs[2:6], refs[6:9], refs[9:]
    (
        order, z1, swapped, z2, zl_in, send_a, send_b, own_a, own_b,
        back_q, back_p, got_q, got_p, wide_q, wide_p, z2_back, unswapped,
        table_sem, sems, line_send, plane_send, few_send,
    ) = refs
    energy, zh = lax.axis_index("energy"), lax.axis_index("elem")
    w, zl = energy // 8 * 2 + energy % 2, energy // 2 % DEPTH
    z = zh * DEPTH + zl
    parts = (0, 1)

    def device(plane, low, high):
        return {"energy": plane // 2 * 8 + low * 2 + plane % 2, "elem": high}

    def line_peer(i):
        other = (z + LINE + (LINE // 2 - (i + 1) // 2) * (1 - 2 * (i % 2))) % LINE
        return other % DEPTH, other // DEPTH

    def far(t):
        return (54 >> (2 * t)) % 4

    def plane_peer(i):
        y = (w // 8 + far(i // 8)) % 4
        x = (w // 2 + far(i // 2 % 4)) % 4
        return y * 8 + x * 2 + (w + 1 + i) % 2

    def meet_zl(low):
        return (low + 2) % DEPTH

    def meet_zh(low, h):
        return (h + (low + 2) // DEPTH) % GROUPS

    def met_quarter(low, high):
        return (high + GROUPS - (3 - low) // 2) % GROUPS

    barrier = pltpu.get_barrier_semaphore()

    def greet_line(i, c):
        low, high = line_peer(i)
        pl.semaphore_signal(barrier, inc=1, device_id=device(w, low, high), device_id_type=MESH)
        return c

    def greet_plane(i, c):
        pl.semaphore_signal(
            barrier, inc=1, device_id=device(plane_peer(i), zl, zh), device_id_type=MESH
        )
        return c

    lax.fori_loop(0, LINE - 1, greet_line, 0)
    lax.fori_loop(0, PLANE - 1, greet_plane, 0)
    table_copies = [
        pltpu.make_async_copy(src, dst, table_sem.at[i])
        for i, (src, dst) in enumerate(zip(tables_in, tables_here))
    ]
    for copy in table_copies:
        copy.start()
    pl.semaphore_wait(barrier, LINE - 1 + PLANE - 1)

    def remote(src, dst, send, recv, where):
        return pltpu.make_async_remote_copy(
            src_ref=src, dst_ref=dst, send_sem=send, recv_sem=recv,
            device_id=where, device_id_type=MESH,
        )

    def arrived(whole, sem):
        pltpu.make_async_copy(whole, whole, sem).wait()

    def quarter(ref, part, h):
        return ref.at[part, pl.ds(pl.multiple_of(h * 8, 8), 8), :]

    def lanes(ref, start, size):
        return ref.at[..., pl.ds(pl.multiple_of(start, LANES), size)]

    started = []

    def send(phase, i, src, dst, recv, where):
        copy = remote(src, dst, few_send.at[phase, i], recv, where)
        copy.start()
        started.append(copy)

    def meet(phase, src, dst, recv):
        for i in range(GROUPS):
            h = (zh + 1 + i) % GROUPS
            send(phase, i, src(h), dst, recv, device(w, meet_zl(zl), meet_zh(zl, h)))

    def leave(phase, src, dst, recv):
        for i in range(GROUPS):
            h = (zh + 1 + i) % GROUPS
            send(phase, i, src(h), dst, recv, device(w, meet_zl(zl), h))

    def depths(phase, src, dst, recv):
        for i in range(DEPTH - 1):
            low = (zl + 1 + i) % DEPTH
            send(phase, i, src(low), dst, recv, device(w, low, zh))
        pltpu.make_async_copy(src(zl), dst, recv).start()

    def line_copy(phase, src, dst, recv, i):
        low, high = line_peer(i)
        return remote(src(low, high), dst, line_send.at[phase, i], recv, device(w, low, high))

    def line(phase, src, dst, recv):
        def start(i, c):
            line_copy(phase, src, dst, recv, i).start()
            return c

        lax.fori_loop(0, LINE - 1, start, 0)
        pltpu.make_async_copy(src(zl, zh), dst, recv).start()

    def line_done(phase, src, dst, recv):
        def done(i, c):
            line_copy(phase, src, dst, recv, i).wait_send()
            return c

        lax.fori_loop(0, LINE - 1, done, 0)

    def plane_copy(phase, src, dst, recv, i):
        other = plane_peer(i)
        return remote(
            src(other), dst(w), plane_send.at[phase, i], recv, device(other, zl, zh)
        )

    def plane(phase, src, dst, recv):
        def start(i, c):
            plane_copy(phase, src, dst, recv, i).start()
            return c

        lax.fori_loop(0, PLANE - 1, start, 0)
        pltpu.make_async_copy(src(w), dst(w), recv).start()

    def plane_done(phase, src, dst, recv):
        def done(i, c):
            plane_copy(phase, src, dst, recv, i).wait_send()
            return c

        lax.fori_loop(0, PLANE - 1, done, 0)

    def both_parts(ref):
        return lambda other: ref.at[:, other]

    def one_part(ref, part):
        return lambda other: ref.at[part, other]

    for i in range(GROUPS):
        h = (zh + 1 + i) % GROUPS
        send(0, i, partner, order.at[zh], sems.at[0], device(w, meet_zl(zl), h))
    for part in parts:
        meet(1 + part, lambda h: quarter(greater, part, h), lanes(z1.at[part], zh * 512, 512), sems.at[1 + part])
    depths(3, lambda low: lanes(lesser, low * LANES, LANES), zl_in.at[zl], sems.at[3])
    arrived(order, sems.at[0])
    flat = order.reshape(LINE, 1, LANES)

    def swapped_src(part):
        return lambda low, high: lanes(swapped.at[part], (high * DEPTH + low) * LANES, LANES)

    def z2_dst(part):
        return z2.at[part, meet_zl(zl), met_quarter(zl, zh)]

    for part in parts:
        arrived(z1.at[part], sems.at[1 + part])
        permute(z1.at[part], swapped.at[part], flat)
        line(part, swapped_src(part), z2_dst(part), sems.at[4 + part])
    for copy in table_copies:
        copy.wait()
    for table, half in zip(tables_here, halves):
        half[0], half[1] = parts_of(table[...])
    arrived(zl_in, sems.at[3])
    for part in parts:
        to_owner(lambda low: zl_in[low, part], send_a.at[part])
    plane(0, both_parts(send_a), both_parts(own_a), sems.at[6])
    for part in parts:
        arrived(z2.at[part], sems.at[4 + part])
        to_owner(lambda low: z2[part, low].reshape(MLOC, LANES), send_b.at[part])
        plane(1 + part, one_part(send_b, part), one_part(own_b, part), sems.at[7 + part])
    arrived(own_a, sems.at[6])
    for part in parts:
        arrived(own_b.at[part], sems.at[7 + part])

    def rows_of(ref):
        return jnp.concatenate([ref[part, :, low, :] for part in parts for low in range(DEPTH)], 0)

    def keep(ref, part, value):
        for low in range(DEPTH):
            ref[part, :, low, :] = value[part * LANES + low * PLANE : part * LANES + (low + 1) * PLANE]

    q, p = correlate(
        rows_of(own_a), rows_of(own_b), *[(half[0], half[1]) for half in halves], tables_here[3]
    )
    for part in parts:
        keep(back_q, part, q)
        plane(3 + part, one_part(back_q, part), one_part(got_q, part), sems.at[9 + part])
    for part in parts:
        keep(back_p, part, p)
    plane(5, both_parts(back_p), both_parts(got_p), sems.at[11])

    def wide_src(part):
        return lambda low, high: wide_q.at[part, meet_zl(low), met_quarter(low, high)]

    def back_dst(part):
        return lanes(z2_back.at[part], z * LANES, LANES)

    for part in parts:
        arrived(got_q.at[part], sems.at[9 + part])

        def keep_q(low, rows):
            wide_q[part, low] = rows.reshape(GROUPS, 8, LANES)

        to_energies(got_q.at[part], keep_q)
        line(2 + part, wide_src(part), back_dst(part), sems.at[12 + part])
    arrived(got_p, sems.at[11])
    for part in parts:

        def keep_p(low, rows):
            wide_p[low, part] = rows

        to_energies(got_p.at[part], keep_p)
    depths(4, lambda low: wide_p.at[low], lanes(lesser_out, zl * LANES, LANES), sems.at[14])
    for part in parts:
        arrived(z2_back.at[part], sems.at[12 + part])
        permute(z2_back.at[part], unswapped.at[part], flat)
        leave(
            5 + part,
            lambda h: lanes(unswapped.at[part], h * 512, 512),
            quarter(greater_out, part, met_quarter(zl, zh)),
            sems.at[15 + part],
        )
    arrived(lesser_out, sems.at[14])
    for part in parts:
        arrived(greater_out.at[part], sems.at[15 + part])
    for copy in started:
        copy.wait_send()
    plane_done(0, both_parts(send_a), both_parts(own_a), sems.at[6])
    plane_done(5, both_parts(back_p), both_parts(got_p), sems.at[11])
    for part in parts:
        line_done(part, swapped_src(part), z2_dst(part), sems.at[4 + part])
        line_done(2 + part, wide_src(part), back_dst(part), sems.at[12 + part])
        plane_done(1 + part, one_part(send_b, part), one_part(own_b, part), sems.at[7 + part])
        plane_done(3 + part, one_part(back_q, part), one_part(got_q, part), sems.at[9 + part])


def per_device(lesser, greater, partner):
    f32 = jnp.float32
    field = jax.ShapeDtypeStruct((2, MLOC, 512), f32)
    owned = pltpu.VMEM((2, PLANE, DEPTH, LANES), f32)
    long = pltpu.VMEM((2, 8, 2048), f32)
    deep = pltpu.VMEM((DEPTH, 2, MLOC, LANES), f32)
    cut = pltpu.VMEM((2, DEPTH, GROUPS, 8, LANES), f32)
    anywhere = pl.BlockSpec(memory_space=pltpu.HBM)
    constants = [jnp.asarray(table) for table in tables()]
    return pl.pallas_call(
        kernel,
        out_shape=(field, field),
        in_specs=[anywhere] * 7,
        out_specs=(anywhere, anywhere),
        scratch_shapes=[
            *[pltpu.VMEM(table.shape, table.dtype) for table in constants],
            *[pltpu.VMEM((2, *table.shape), jnp.bfloat16) for table in constants[:3]],
            pltpu.VMEM((GROUPS, 4, 1, LANES), jnp.int32),
            long, long, cut, deep, owned, owned, owned, owned,
            owned, owned, owned, owned, cut, deep, long, long,
            pltpu.SemaphoreType.DMA((4,)),
            pltpu.SemaphoreType.DMA((17,)),
            pltpu.SemaphoreType.DMA((4, LINE - 1)),
            pltpu.SemaphoreType.DMA((6, PLANE - 1)),
            pltpu.SemaphoreType.DMA((7, 4)),
        ],
        compiler_params=pltpu.CompilerParams(
            collective_id=0, has_side_effects=True, vmem_limit_bytes=56 * 1024 * 1024
        ),
    )(lesser, greater, partner.reshape(4, 1, LANES), *constants)


def solution(mesh):
    placed = (P(None, "energy", "elem"), P(None, "energy", "elem"), P("elem"))
    return jax.shard_map(
        per_device,
        mesh=mesh,
        in_specs=placed,
        out_specs=(P(None, "energy", "elem"), P(None, "energy", "elem")),
        check_vma=False,
    )
```

```python
import jax
import jax.numpy as jnp
import numpy as np
from jax import lax
from jax.experimental import pallas as pl
from jax.experimental.pallas import tpu as pltpu
from jax.sharding import PartitionSpec as P

PLANE, DEPTH, GROUPS, MLOC = 32, 4, 4, 32
LINE = DEPTH * GROUPS
ROWS, LANES = 256, 128
PERIOD = 8192
MESH = pl.DeviceIdType.MESH


def tables():
    row = np.arange(ROWS)
    part, zl, plane = row // LANES, row // PLANE % DEPTH, row % PLANE
    index = plane // 2 * 8 + zl * 2 + plane % 2
    freq = np.arange(ROWS)
    angle = 2 * np.pi * (freq[:, None] * index[None, :] % ROWS) / ROWS
    cos, sin = np.cos(angle), np.sin(angle)
    first = np.concatenate(
        [np.where(part == 0, cos, sin), np.where(part == 0, -sin, cos)], 0
    )
    scale = 1.0 / (64 * PERIOD)
    last = scale * np.concatenate(
        [np.where(part == 0, sin, cos).T, np.where(part == 0, -cos, sin).T], 1
    )
    lane = np.arange(LANES)
    local, el = lane % MLOC, lane // MLOC
    same = (el[:, None] == el[None, :]).astype(np.float64)
    angle = 2 * np.pi * (local[:, None] * local[None, :] % MLOC) / MLOC
    cos, sin = same * np.cos(angle), same * np.sin(angle)
    middle = np.block([[cos, -sin], [sin, cos]])
    angle = 2 * np.pi * (freq[:, None] * local[None, :]) / PERIOD
    turn = np.stack([np.cos(angle), np.sin(angle)]).astype(np.float32)
    return [*(table.astype(np.float32) for table in (first, middle, last)), turn]


def parts_of(x):
    high = x.astype(jnp.bfloat16)
    return high, (x - high.astype(jnp.float32)).astype(jnp.bfloat16)


def mm(a, b):
    return jnp.dot(a, b, preferred_element_type=jnp.float32)


def table_times(table, x):
    high, low = table
    xh, xl = parts_of(x)
    return mm(high, xh) + (mm(high, xl) + mm(low, xh))


def times_table(x, table):
    high, low = table
    xh, xl = parts_of(x)
    return mm(xh, high) + (mm(xl, high) + mm(xh, low))


def turned(real, imag, cos, sin):
    return real * cos + imag * sin, imag * cos - real * sin


def both(left, right):
    return jnp.concatenate([left, right], axis=1)


def forward(rows, first, middle, cos, sin):
    y = table_times(first, rows)
    return times_table(both(*turned(y[:ROWS], y[ROWS:], cos, sin)), middle)


def conjugate(z):
    return both(z[:, :LANES], -z[:, LANES:])


def product(a, b):
    ar, ai, br, bi = a[:, :LANES], a[:, LANES:], b[:, :LANES], b[:, LANES:]
    return both(ar * br + ai * bi, ai * br - ar * bi)


def inverse(z, middle, last, cos, sin):
    v = times_table(z, middle)
    return table_times(last, jnp.concatenate(turned(v[:, :LANES], v[:, LANES:], cos, sin), 0))


def blocks_swapped(t):
    cut = [[t[32 * i : 32 * i + 32, 32 * j : 32 * j + 32] for j in range(4)] for i in range(4)]
    return [jnp.concatenate([cut[i][j] for i in range(4)], axis=1) for j in range(4)]


def to_owner(block, out):
    t = jnp.concatenate([block(zl) for zl in range(DEPTH)], 0).T
    for zl, rows in enumerate(blocks_swapped(t)):
        out[:, zl, :] = rows


def to_energies(got, store):
    rows = jnp.concatenate([got[:, zl, :] for zl in range(DEPTH)], 0)
    t = jnp.concatenate(blocks_swapped(rows), 0).T
    for zl in range(DEPTH):
        store(zl, t[MLOC * zl : MLOC * zl + MLOC])


def permuted(src, order, d):
    at = jnp.broadcast_to(order[d], (8, LANES))
    lane, where = at % LANES, at // LANES
    total = jnp.take_along_axis(src[:, :LANES], lane, axis=1)
    for s in range(1, LINE):
        moved = jnp.take_along_axis(src[:, s * LANES : (s + 1) * LANES], lane, axis=1)
        total = jnp.where(where == s, moved, total)
    return total


def kernel(
    lesser, greater, partner, *refs,
):
    tables_in, refs = refs[:4], refs[4:]
    lesser_out, greater_out = refs[:2]
    tables_here, halves, refs = refs[2:6], refs[6:9], refs[9:]
    (
        order, z1, swapped, z2, lesser_here, send_a, mid_a, deep_a, own_a, freq_a, send_b, own_b,
        back_q, got_q, wide_q, z2_back, unswapped, freq_p, back_p, mid_p, send_p, got_p, lesser_done,
        table_sem, sems, line_send, plane_send, few_send,
    ) = refs
    energy, zh = lax.axis_index("energy"), lax.axis_index("elem")
    w, zl = energy // 8 * 2 + energy % 2, energy // 2 % DEPTH
    z = zh * DEPTH + zl
    parts = (0, 1)

    def device(plane, low, high):
        return {"energy": plane // 2 * 8 + low * 2 + plane % 2, "elem": high}

    def line_peer(i):
        other = (z + LINE + (LINE // 2 - (i + 1) // 2) * (1 - 2 * (i % 2))) % LINE
        return other % DEPTH, other // DEPTH

    def far(t):
        return (54 >> (2 * t)) % 4

    def plane_peer(i):
        y = (w // 8 + far(i // 8)) % 4
        x = (w // 2 + far(i // 2 % 4)) % 4
        return y * 8 + x * 2 + (w + 1 + i) % 2

    def meet_zl(low):
        return (low + 2) % DEPTH

    def meet_zh(low, h):
        return (h + (low + 2) // DEPTH) % GROUPS

    def met_quarter(low, high):
        return (high + GROUPS - (3 - low) // 2) % GROUPS

    barrier = pltpu.get_barrier_semaphore()

    def greet_line(i, c):
        low, high = line_peer(i)
        pl.semaphore_signal(barrier, inc=1, device_id=device(w, low, high), device_id_type=MESH)
        return c

    def greet_plane(i, c):
        pl.semaphore_signal(
            barrier, inc=1, device_id=device(plane_peer(i), zl, zh), device_id_type=MESH
        )
        return c

    lax.fori_loop(0, LINE - 1, greet_line, 0)
    lax.fori_loop(0, PLANE - 1, greet_plane, 0)
    table_copies = [
        pltpu.make_async_copy(src, dst, table_sem.at[i])
        for i, (src, dst) in enumerate(zip(tables_in, tables_here))
    ]
    for copy in table_copies:
        copy.start()
    lesser_copy = pltpu.make_async_copy(lesser, lesser_here, table_sem.at[4])
    lesser_copy.start()
    lesser_copy.wait()
    for part in parts:
        to_owner(lambda low: lesser_here[part, :, low * LANES : (low + 1) * LANES], send_a.at[part])
    pl.semaphore_wait(barrier, LINE - 1 + PLANE - 1)

    def remote(src, dst, send, recv, where):
        return pltpu.make_async_remote_copy(
            src_ref=src, dst_ref=dst, send_sem=send, recv_sem=recv,
            device_id=where, device_id_type=MESH,
        )

    def arrived(whole, sem):
        pltpu.make_async_copy(whole, whole, sem).wait()

    def quarter(ref, part, h):
        return ref.at[part, pl.ds(pl.multiple_of(h * 8, 8), 8), :]

    def lanes(ref, start, size):
        return ref.at[..., pl.ds(pl.multiple_of(start, LANES), size)]

    started = []

    def send(phase, i, src, dst, recv, where):
        copy = remote(src, dst, few_send.at[phase, i], recv, where)
        copy.start()
        started.append(copy)

    def meet(phase, src, dst, recv):
        for i in range(GROUPS):
            h = (zh + 1 + i) % GROUPS
            send(phase, i, src(h), dst, recv, device(w, meet_zl(zl), meet_zh(zl, h)))

    def depths(phase, src, dst, recv):
        for i in range(DEPTH - 1):
            low = (zl + 1 + i) % DEPTH
            send(phase, i, src(low), dst, recv, device(w, low, zh))
        pltpu.make_async_copy(src(zl), dst, recv).start()

    def line_copy(phase, src, dst, recv, i):
        low, high = line_peer(i)
        return remote(src(low, high), dst, line_send.at[phase, i], recv, device(w, low, high))

    def line(phase, src, dst, recv, make=None):
        def start(i, c):
            if make is not None:
                make(*line_peer(i))
            line_copy(phase, src, dst, recv, i).start()
            return c

        lax.fori_loop(0, LINE - 1, start, 0, unroll=3)
        if make is not None:
            make(zl, zh)
        pltpu.make_async_copy(src(zl, zh), dst, recv).start()

    def line_done(phase, src, dst, recv):
        def done(i, c):
            line_copy(phase, src, dst, recv, i).wait_send()
            return c

        lax.fori_loop(0, LINE - 1, done, 0)

    def plane_copy(phase, src, dst, recv, i):
        other = plane_peer(i)
        return remote(
            src(other), dst(w), plane_send.at[phase, i], recv, device(other, zl, zh)
        )

    def plane(phase, src, dst, recv):
        def start(i, c):
            plane_copy(phase, src, dst, recv, i).start()
            return c

        lax.fori_loop(0, PLANE - 1, start, 0, unroll=4)
        pltpu.make_async_copy(src(w), dst(w), recv).start()

    def plane_done(phase, src, dst, recv):
        def done(i, c):
            plane_copy(phase, src, dst, recv, i).wait_send()
            return c

        lax.fori_loop(0, PLANE - 1, done, 0)

    def both_parts(ref):
        return lambda other: ref.at[:, other]

    def one_part(ref, part):
        return lambda other: ref.at[part, other]

    def make_tile(src, dst):
        def make(low, high):
            d = high * DEPTH + low
            dst[:, pl.ds(pl.multiple_of(d * LANES, LANES), LANES)] = permuted(src, flat, d)

        return make

    for i in range(GROUPS):
        h = (zh + 1 + i) % GROUPS
        send(0, i, partner, order.at[zh], sems.at[0], device(w, meet_zl(zl), h))
    for part in parts:
        meet(1 + part, lambda h: quarter(greater, part, h), lanes(z1.at[part], zh * 512, 512), sems.at[1 + part])
    plane(0, both_parts(send_a), both_parts(mid_a), sems.at[6])
    for copy in table_copies:
        copy.wait()
    for table, half in zip(tables_here, halves):
        half[0], half[1] = parts_of(table[...])
    first, middle, last = [lambda half=half: (half[0], half[1]) for half in halves]
    turn = tables_here[3]
    arrived(order, sems.at[0])
    flat = order.reshape(LINE, 1, LANES)

    def swapped_src(part):
        return lambda low, high: lanes(swapped.at[part], (high * DEPTH + low) * LANES, LANES)

    def z2_dst(part):
        return z2.at[part, meet_zl(zl), met_quarter(zl, zh)]

    for part in parts:
        arrived(z1.at[part], sems.at[1 + part])
        line(part, swapped_src(part), z2_dst(part), sems.at[4 + part], make_tile(z1.at[part], swapped.at[part]))
    arrived(mid_a, sems.at[6])
    for low in range(DEPTH):
        for part in parts:
            deep_a[low, part] = mid_a[part, :, low, :]
    depths(3, lambda low: deep_a.at[low], own_a.at[:, zl], sems.at[3])
    for part in parts:
        arrived(z2.at[part], sems.at[4 + part])
        to_owner(lambda low: z2[part, low].reshape(MLOC, LANES), send_b.at[part])
        plane(1 + part, one_part(send_b, part), one_part(own_b, part), sems.at[7 + part])
    arrived(own_a, sems.at[3])
    freq_a[...] = forward(own_a[...].reshape(ROWS, LANES), first(), middle(), turn[0], turn[1])
    for part in parts:
        arrived(own_b.at[part], sems.at[7 + part])
    rows_b = jnp.concatenate(
        [(own_b[part, :, low, :] if part == 0 else -own_b[part, :, low, :]) for part in parts for low in range(DEPTH)], 0
    )
    joint = product(freq_a[...], forward(rows_b, first(), middle(), turn[0], turn[1]))
    freq_p[...] = conjugate(joint)
    q = inverse(joint, middle(), last(), turn[0], turn[1])
    for part in parts:
        for low in range(DEPTH):
            back_q[part, :, low, :] = q[part * LANES + low * PLANE : part * LANES + (low + 1) * PLANE]
        plane(3 + part, one_part(back_q, part), one_part(got_q, part), sems.at[9 + part])
    p = inverse(freq_p[...], middle(), last(), turn[0], turn[1])
    for low in range(DEPTH):
        back_p[low, 0] = -p[low * PLANE : (low + 1) * PLANE]
        back_p[low, 1] = p[LANES + low * PLANE : LANES + (low + 1) * PLANE]
    depths(4, lambda low: back_p.at[low], mid_p.at[:, zl], sems.at[14])

    def wide_src(part):
        return lambda low, high: wide_q.at[part, meet_zl(low), met_quarter(low, high)]

    def back_dst(part):
        return lanes(z2_back.at[part], z * LANES, LANES)

    for part in parts:
        arrived(got_q.at[part], sems.at[9 + part])

        def keep_q(low, rows):
            wide_q[part, low] = rows.reshape(GROUPS, 8, LANES)

        to_energies(got_q.at[part], keep_q)
        line(2 + part, wide_src(part), back_dst(part), sems.at[12 + part])
    arrived(mid_p, sems.at[14])
    for part in parts:
        for low in range(DEPTH):
            send_p[part, :, low, :] = mid_p[part, low]
    plane(5, both_parts(send_p), both_parts(got_p), sems.at[11])
    for part in parts:
        arrived(z2_back.at[part], sems.at[12 + part])
        make = make_tile(z2_back.at[part], unswapped.at[part])
        for i in range(GROUPS):
            h = (zh + 1 + i) % GROUPS
            for low in range(DEPTH):
                make(low, h)
            send(
                5 + part, i, lanes(unswapped.at[part], h * 512, 512),
                quarter(greater_out, part, met_quarter(zl, zh)), sems.at[15 + part],
                device(w, meet_zl(zl), h),
            )
    arrived(got_p, sems.at[11])
    for part in parts:

        def keep_p(low, rows):
            lesser_done[part, :, low * LANES : (low + 1) * LANES] = rows

        to_energies(got_p.at[part], keep_p)
    lesser_copy = pltpu.make_async_copy(lesser_done, lesser_out, table_sem.at[5])
    lesser_copy.start()
    for copy in started:
        copy.wait_send()
    plane_done(0, both_parts(send_a), both_parts(mid_a), sems.at[6])
    plane_done(5, both_parts(send_p), both_parts(got_p), sems.at[11])
    for part in parts:
        line_done(part, swapped_src(part), z2_dst(part), sems.at[4 + part])
        line_done(2 + part, wide_src(part), back_dst(part), sems.at[12 + part])
        plane_done(1 + part, one_part(send_b, part), one_part(own_b, part), sems.at[7 + part])
        plane_done(3 + part, one_part(back_q, part), one_part(got_q, part), sems.at[9 + part])
    lesser_copy.wait()
    for part in parts:
        arrived(greater_out.at[part], sems.at[15 + part])


def per_device(lesser, greater, partner):
    f32 = jnp.float32
    field = jax.ShapeDtypeStruct((2, MLOC, 512), f32)
    owned = pltpu.VMEM((2, PLANE, DEPTH, LANES), f32)
    long = pltpu.VMEM((2, 8, 2048), f32)
    whole = pltpu.VMEM((2, MLOC, 512), f32)
    deep = pltpu.VMEM((DEPTH, 2, PLANE, LANES), f32)
    sorted_ = pltpu.VMEM((2, DEPTH, PLANE, LANES), f32)
    freq = pltpu.VMEM((ROWS, ROWS), f32)
    cut = pltpu.VMEM((2, DEPTH, GROUPS, 8, LANES), f32)
    anywhere = pl.BlockSpec(memory_space=pltpu.HBM)
    constants = [jnp.asarray(table) for table in tables()]
    return pl.pallas_call(
        kernel,
        out_shape=(field, field),
        in_specs=[anywhere] * 7,
        out_specs=(anywhere, anywhere),
        scratch_shapes=[
            *[pltpu.VMEM(table.shape, table.dtype) for table in constants],
            *[pltpu.VMEM((2, *table.shape), jnp.bfloat16) for table in constants[:3]],
            pltpu.VMEM((GROUPS, 4, 1, LANES), jnp.int32),
            long, long, cut, whole, owned, owned, deep, sorted_, freq, owned, owned,
            owned, owned, cut, long, long, freq, deep, sorted_, owned, owned, whole,
            pltpu.SemaphoreType.DMA((6,)),
            pltpu.SemaphoreType.DMA((17,)),
            pltpu.SemaphoreType.DMA((4, LINE - 1)),
            pltpu.SemaphoreType.DMA((6, PLANE - 1)),
            pltpu.SemaphoreType.DMA((7, 4)),
        ],
        compiler_params=pltpu.CompilerParams(
            collective_id=0, has_side_effects=True, vmem_limit_bytes=56 * 1024 * 1024
        ),
    )(lesser, greater, partner.reshape(4, 1, LANES), *constants)


def solution(mesh):
    placed = (P(None, "energy", "elem"), P(None, "energy", "elem"), P("elem"))
    return jax.shard_map(
        per_device,
        mesh=mesh,
        in_specs=placed,
        out_specs=(P(None, "energy", "elem"), P(None, "energy", "elem")),
        check_vma=False,
    )
```

```python
import jax
import jax.numpy as jnp
import numpy as np
from jax import lax
from jax.experimental import pallas as pl
from jax.experimental.pallas import tpu as pltpu
from jax.sharding import PartitionSpec as P

PLANE, DEPTH, GROUPS, MLOC = 32, 4, 4, 32
LINE = DEPTH * GROUPS
ROWS, LANES = 256, 128
PERIOD = 8192
MESH = pl.DeviceIdType.MESH
HOPS = (0, 1, 2, 1)
PLANE_STEPS = sorted(range(1, PLANE), key=lambda k: -HOPS[k >> 3] - HOPS[k >> 1 & 3])
LINE_STEPS = (8, 9, 10, 11, 7, 6, 14, 13, 5, 12, 4, 15, 3, 2, 1)


def tables():
    row = np.arange(ROWS)
    part, zl, plane = row // LANES, row // PLANE % DEPTH, row % PLANE
    index = plane // 2 * 8 + zl * 2 + plane % 2
    freq = np.arange(ROWS)
    angle = 2 * np.pi * (freq[:, None] * index[None, :] % ROWS) / ROWS
    cos, sin = np.cos(angle), np.sin(angle)
    first = np.concatenate(
        [np.where(part == 0, cos, sin), np.where(part == 0, -sin, cos)], 0
    )
    scale = 1.0 / (64 * PERIOD)
    last = scale * np.concatenate(
        [np.where(part == 0, sin, cos).T, np.where(part == 0, -cos, sin).T], 1
    )
    lane = np.arange(LANES)
    local, el = lane % MLOC, lane // MLOC
    same = (el[:, None] == el[None, :]).astype(np.float64)
    angle = 2 * np.pi * (local[:, None] * local[None, :] % MLOC) / MLOC
    cos, sin = same * np.cos(angle), same * np.sin(angle)
    middle = np.block([[cos, -sin], [sin, cos]])
    angle = 2 * np.pi * (freq[:, None] * local[None, :]) / PERIOD
    turn = np.stack([np.cos(angle), np.sin(angle)]).astype(np.float32)
    return [*(table.astype(np.float32) for table in (first, middle, last)), turn]


def parts_of(x):
    high = x.astype(jnp.bfloat16)
    return high, (x - high.astype(jnp.float32)).astype(jnp.bfloat16)


def mm(a, b):
    return jnp.dot(a, b, preferred_element_type=jnp.float32)


def table_times(table, x):
    high, low = table
    xh, xl = parts_of(x)
    return mm(high, xh) + (mm(high, xl) + mm(low, xh))


def times_table(x, table):
    high, low = table
    xh, xl = parts_of(x)
    return mm(xh, high) + (mm(xl, high) + mm(xh, low))


def turned(real, imag, cos, sin):
    return real * cos + imag * sin, imag * cos - real * sin


def both(left, right):
    return jnp.concatenate([left, right], axis=1)


def forward(rows, first, middle, cos, sin):
    y = table_times(first, rows)
    return times_table(both(*turned(y[:ROWS], y[ROWS:], cos, sin)), middle)


def conjugate(z):
    return both(z[:, :LANES], -z[:, LANES:])


def product(a, b):
    ar, ai, br, bi = a[:, :LANES], a[:, LANES:], b[:, :LANES], b[:, LANES:]
    return both(ar * br + ai * bi, ai * br - ar * bi)


def inverse(z, middle, last, cos, sin):
    v = times_table(z, middle)
    return table_times(last, jnp.concatenate(turned(v[:, :LANES], v[:, LANES:], cos, sin), 0))


def blocks_swapped(t):
    cut = [[t[32 * i : 32 * i + 32, 32 * j : 32 * j + 32] for j in range(4)] for i in range(4)]
    return [jnp.concatenate([cut[i][j] for i in range(4)], axis=1) for j in range(4)]


def to_owner(block, out):
    t = jnp.concatenate([block(zl) for zl in range(DEPTH)], 0).T
    for zl, rows in enumerate(blocks_swapped(t)):
        out[:, zl, :] = rows


def to_energies(got, store):
    rows = jnp.concatenate([got[:, zl, :] for zl in range(DEPTH)], 0)
    t = jnp.concatenate(blocks_swapped(rows), 0).T
    for zl in range(DEPTH):
        store(zl, t[MLOC * zl : MLOC * zl + MLOC])


def permuted(src, order, d):
    at = jnp.broadcast_to(order[d], (8, LANES))
    lane, where = at % LANES, at // LANES
    total = jnp.take_along_axis(src[:, :LANES], lane, axis=1)
    for s in range(1, LINE):
        moved = jnp.take_along_axis(src[:, s * LANES : (s + 1) * LANES], lane, axis=1)
        total = jnp.where(where == s, moved, total)
    return total


def kernel(
    lesser, greater, partner, *refs,
):
    tables_in, refs = refs[:4], refs[4:]
    lesser_out, greater_out = refs[:2]
    tables_here, halves, refs = refs[2:6], refs[6:9], refs[9:]
    (
        order, z1, swapped, z2, lesser_here, send_a, mid_a, deep_a, own_a, freq_a, send_b, own_b,
        back_q, got_q, wide_q, z2_back, unswapped, freq_p, back_p, mid_p, send_p, got_p, lesser_done,
        table_sem, sems, line_send, plane_send, few_send,
    ) = refs
    energy, zh = lax.axis_index("energy"), lax.axis_index("elem")
    w, zl = energy // 8 * 2 + energy % 2, energy // 2 % DEPTH
    z = zh * DEPTH + zl
    parts = (0, 1)

    def device(plane, low, high):
        return {"energy": plane // 2 * 8 + low * 2 + plane % 2, "elem": high}

    def line_peer(i):
        other = (z + LINE + (LINE // 2 - (i + 1) // 2) * (1 - 2 * (i % 2))) % LINE
        return other % DEPTH, other // DEPTH

    def flips(value, *weights):
        return [weight * (1 - 2 * (value // weight % 2)) for weight in weights]

    def flipped(value, steps, k):
        return value + sum(step for bit, step in enumerate(steps) if k >> bit & 1)

    plane_flips, w_flips = flips(energy, 1, 8, 16, 32, 64), flips(w, 1, 2, 4, 8, 16)
    depth_flips, zl_flips, zh_flips = flips(energy, 2, 4), flips(zl, 1, 2), flips(zh, 1, 2)
    plane_peers = [
        (flipped(w, w_flips, k), {"energy": flipped(energy, plane_flips, k), "elem": zh})
        for k in PLANE_STEPS
    ]
    line_peers = [
        (
            flipped(zl, zl_flips, k % 4),
            flipped(zh, zh_flips, k // 4),
            {"energy": flipped(energy, depth_flips, k % 4), "elem": flipped(zh, zh_flips, k // 4)},
        )
        for k in LINE_STEPS
    ]

    def meet_zl(low):
        return (low + 2) % DEPTH

    def meet_zh(low, h):
        return (h + (low + 2) // DEPTH) % GROUPS

    def met_quarter(low, high):
        return (high + GROUPS - (3 - low) // 2) % GROUPS

    barrier = pltpu.get_barrier_semaphore()

    for *_, where in line_peers + plane_peers:
        pl.semaphore_signal(barrier, inc=1, device_id=where, device_id_type=MESH)
    table_copies = [
        pltpu.make_async_copy(src, dst, table_sem.at[i])
        for i, (src, dst) in enumerate(zip(tables_in, tables_here))
    ]
    for copy in table_copies:
        copy.start()
    lesser_copy = pltpu.make_async_copy(lesser, lesser_here, table_sem.at[4])
    lesser_copy.start()
    lesser_copy.wait()
    for part in parts:
        to_owner(lambda low: lesser_here[part, :, low * LANES : (low + 1) * LANES], send_a.at[part])
    pl.semaphore_wait(barrier, LINE - 1 + PLANE - 1)

    def remote(src, dst, send, recv, where):
        return pltpu.make_async_remote_copy(
            src_ref=src, dst_ref=dst, send_sem=send, recv_sem=recv,
            device_id=where, device_id_type=MESH,
        )

    def arrived(whole, sem):
        pltpu.make_async_copy(whole, whole, sem).wait()

    def quarter(ref, part, h):
        return ref.at[part, pl.ds(pl.multiple_of(h * 8, 8), 8), :]

    def lanes(ref, start, size):
        return ref.at[..., pl.ds(pl.multiple_of(start, LANES), size)]

    started = []

    def send(phase, i, src, dst, recv, where):
        copy = remote(src, dst, few_send.at[phase, i], recv, where)
        copy.start()
        started.append(copy)

    def meet(phase, src, dst, recv):
        for i in range(GROUPS):
            h = (zh + 1 + i) % GROUPS
            send(phase, i, src(h), dst, recv, device(w, meet_zl(zl), meet_zh(zl, h)))

    def depths(phase, src, dst, recv):
        for i in range(DEPTH - 1):
            low = (zl + 1 + i) % DEPTH
            send(phase, i, src(low), dst, recv, device(w, low, zh))
        pltpu.make_async_copy(src(zl), dst, recv).start()

    def line(phase, src, dst, recv, make=None):
        if make is None:
            for low, high, where in line_peers:
                remote(src(low, high), dst, line_send.at[phase], recv, where).start()
        else:

            def start(i, c):
                low, high = line_peer(i)
                make(low, high)
                remote(
                    src(low, high), dst, line_send.at[phase], recv, device(w, low, high)
                ).start()
                return c

            lax.fori_loop(0, LINE - 1, start, 0, unroll=3)
            make(zl, zh)
        pltpu.make_async_copy(src(zl, zh), dst, recv).start()

    def line_done(phase):
        arrived(swapped.at[0, :, pl.ds(0, (LINE - 1) * LANES)], line_send.at[phase])

    def plane(phase, src, dst, recv):
        for other, where in plane_peers:
            remote(src(other), dst(w), plane_send.at[phase], recv, where).start()
        pltpu.make_async_copy(src(w), dst(w), recv).start()

    def plane_done(phase, blocks):
        arrived(blocks, plane_send.at[phase])

    def both_parts(ref):
        return lambda other: ref.at[:, other]

    def one_part(ref, part):
        return lambda other: ref.at[part, other]

    def make_tile(src, dst):
        def make(low, high):
            d = high * DEPTH + low
            dst[:, pl.ds(pl.multiple_of(d * LANES, LANES), LANES)] = permuted(src, flat, d)

        return make

    for i in range(GROUPS):
        h = (zh + 1 + i) % GROUPS
        send(0, i, partner, order.at[zh], sems.at[0], device(w, meet_zl(zl), h))
    for part in parts:
        meet(1 + part, lambda h: quarter(greater, part, h), lanes(z1.at[part], zh * 512, 512), sems.at[1 + part])
    plane(0, both_parts(send_a), both_parts(mid_a), sems.at[6])
    for copy in table_copies:
        copy.wait()
    for table, half in zip(tables_here, halves):
        half[0], half[1] = parts_of(table[...])
    first, middle, last = [lambda half=half: (half[0], half[1]) for half in halves]
    turn = tables_here[3]
    arrived(order, sems.at[0])
    flat = order.reshape(LINE, 1, LANES)

    def swapped_src(part):
        return lambda low, high: lanes(swapped.at[part], (high * DEPTH + low) * LANES, LANES)

    def z2_dst(part):
        return z2.at[part, meet_zl(zl), met_quarter(zl, zh)]

    for part in parts:
        arrived(z1.at[part], sems.at[1 + part])
        line(part, swapped_src(part), z2_dst(part), sems.at[4 + part], make_tile(z1.at[part], swapped.at[part]))
    arrived(mid_a, sems.at[6])
    for low in range(DEPTH):
        for part in parts:
            deep_a[low, part] = mid_a[part, :, low, :]
    depths(3, lambda low: deep_a.at[low], own_a.at[:, zl], sems.at[3])
    for part in parts:
        arrived(z2.at[part], sems.at[4 + part])
        to_owner(lambda low: z2[part, low].reshape(MLOC, LANES), send_b.at[part])
        plane(1 + part, one_part(send_b, part), one_part(own_b, part), sems.at[7 + part])
    arrived(own_a, sems.at[3])
    freq_a[...] = forward(own_a[...].reshape(ROWS, LANES), first(), middle(), turn[0], turn[1])
    for part in parts:
        arrived(own_b.at[part], sems.at[7 + part])
    rows_b = jnp.concatenate(
        [(own_b[part, :, low, :] if part == 0 else -own_b[part, :, low, :]) for part in parts for low in range(DEPTH)], 0
    )
    joint = product(freq_a[...], forward(rows_b, first(), middle(), turn[0], turn[1]))
    freq_p[...] = conjugate(joint)
    q = inverse(joint, middle(), last(), turn[0], turn[1])
    for part in parts:
        for low in range(DEPTH):
            back_q[part, :, low, :] = q[part * LANES + low * PLANE : part * LANES + (low + 1) * PLANE]
        plane(3 + part, one_part(back_q, part), one_part(got_q, part), sems.at[9 + part])
    p = inverse(freq_p[...], middle(), last(), turn[0], turn[1])
    for low in range(DEPTH):
        back_p[low, 0] = -p[low * PLANE : (low + 1) * PLANE]
        back_p[low, 1] = p[LANES + low * PLANE : LANES + (low + 1) * PLANE]
    depths(4, lambda low: back_p.at[low], mid_p.at[:, zl], sems.at[14])

    def wide_src(part):
        return lambda low, high: wide_q.at[part, meet_zl(low), met_quarter(low, high)]

    def back_dst(part):
        return lanes(z2_back.at[part], z * LANES, LANES)

    for part in parts:
        arrived(got_q.at[part], sems.at[9 + part])

        def keep_q(low, rows):
            wide_q[part, low] = rows.reshape(GROUPS, 8, LANES)

        to_energies(got_q.at[part], keep_q)
        line(2 + part, wide_src(part), back_dst(part), sems.at[12 + part])
    arrived(mid_p, sems.at[14])
    for part in parts:
        for low in range(DEPTH):
            send_p[part, :, low, :] = mid_p[part, low]
    plane(5, both_parts(send_p), both_parts(got_p), sems.at[11])
    for part in parts:
        arrived(z2_back.at[part], sems.at[12 + part])
        make = make_tile(z2_back.at[part], unswapped.at[part])
        for i in range(GROUPS):
            h = (zh + 1 + i) % GROUPS
            for low in range(DEPTH):
                make(low, h)
            send(
                5 + part, i, lanes(unswapped.at[part], h * 512, 512),
                quarter(greater_out, part, met_quarter(zl, zh)), sems.at[15 + part],
                device(w, meet_zl(zl), h),
            )
    arrived(got_p, sems.at[11])
    for part in parts:

        def keep_p(low, rows):
            lesser_done[part, :, low * LANES : (low + 1) * LANES] = rows

        to_energies(got_p.at[part], keep_p)
    lesser_copy = pltpu.make_async_copy(lesser_done, lesser_out, table_sem.at[5])
    lesser_copy.start()
    for copy in started:
        copy.wait_send()
    plane_done(0, send_a.at[:, pl.ds(0, PLANE - 1)])
    plane_done(5, send_p.at[:, pl.ds(0, PLANE - 1)])
    for part in parts:
        line_done(part)
        line_done(2 + part)
        plane_done(1 + part, send_b.at[part, pl.ds(0, PLANE - 1)])
        plane_done(3 + part, back_q.at[part, pl.ds(0, PLANE - 1)])
    lesser_copy.wait()
    for part in parts:
        arrived(greater_out.at[part], sems.at[15 + part])


def per_device(lesser, greater, partner):
    f32 = jnp.float32
    field = jax.ShapeDtypeStruct((2, MLOC, 512), f32)
    owned = pltpu.VMEM((2, PLANE, DEPTH, LANES), f32)
    long = pltpu.VMEM((2, 8, 2048), f32)
    whole = pltpu.VMEM((2, MLOC, 512), f32)
    deep = pltpu.VMEM((DEPTH, 2, PLANE, LANES), f32)
    sorted_ = pltpu.VMEM((2, DEPTH, PLANE, LANES), f32)
    freq = pltpu.VMEM((ROWS, ROWS), f32)
    cut = pltpu.VMEM((2, DEPTH, GROUPS, 8, LANES), f32)
    anywhere = pl.BlockSpec(memory_space=pltpu.HBM)
    constants = [jnp.asarray(table) for table in tables()]
    return pl.pallas_call(
        kernel,
        out_shape=(field, field),
        in_specs=[anywhere] * 7,
        out_specs=(anywhere, anywhere),
        scratch_shapes=[
            *[pltpu.VMEM(table.shape, table.dtype) for table in constants],
            *[pltpu.VMEM((2, *table.shape), jnp.bfloat16) for table in constants[:3]],
            pltpu.VMEM((GROUPS, 4, 1, LANES), jnp.int32),
            long, long, cut, whole, owned, owned, deep, sorted_, freq, owned, owned,
            owned, owned, cut, long, long, freq, deep, sorted_, owned, owned, whole,
            pltpu.SemaphoreType.DMA((6,)),
            pltpu.SemaphoreType.DMA((17,)),
            pltpu.SemaphoreType.DMA((4,)),
            pltpu.SemaphoreType.DMA((6,)),
            pltpu.SemaphoreType.DMA((7, 4)),
        ],
        compiler_params=pltpu.CompilerParams(
            collective_id=0, has_side_effects=True, vmem_limit_bytes=56 * 1024 * 1024
        ),
    )(lesser, greater, partner.reshape(4, 1, LANES), *constants)


def solution(mesh):
    placed = (P(None, "energy", "elem"), P(None, "energy", "elem"), P("elem"))
    return jax.shard_map(
        per_device,
        mesh=mesh,
        in_specs=placed,
        out_specs=(P(None, "energy", "elem"), P(None, "energy", "elem")),
        check_vma=False,
    )
```

```python
import jax
import jax.numpy as jnp
import numpy as np
from jax import lax
from jax.experimental import pallas as pl
from jax.experimental.pallas import tpu as pltpu
from jax.sharding import PartitionSpec as P

PLANE, DEPTH, GROUPS, MLOC = 32, 4, 4, 32
LINE = DEPTH * GROUPS
ROWS, LANES = 256, 128
PERIOD = 8192
MESH = pl.DeviceIdType.MESH
HOPS = (0, 1, 2, 1)
PLANE_STEPS = sorted(range(1, PLANE), key=lambda k: -HOPS[k >> 3] - HOPS[k >> 1 & 3])
LINE_STEPS = (8, 9, 10, 11, 7, 6, 14, 13, 5, 12, 4, 15, 3, 2, 1)


def tables():
    row = np.arange(ROWS)
    part, zl, plane = row // LANES, row // PLANE % DEPTH, row % PLANE
    index = plane // 2 * 8 + zl * 2 + plane % 2
    freq = np.arange(ROWS)
    angle = 2 * np.pi * (freq[:, None] * index[None, :] % ROWS) / ROWS
    cos, sin = np.cos(angle), np.sin(angle)
    first = np.concatenate(
        [np.where(part == 0, cos, sin), np.where(part == 0, -sin, cos)], 0
    )
    scale = 1.0 / (64 * PERIOD)
    last = scale * np.concatenate(
        [np.where(part == 0, sin, cos).T, np.where(part == 0, -cos, sin).T], 1
    )
    lane = np.arange(LANES)
    local, el = lane % MLOC, lane // MLOC
    same = (el[:, None] == el[None, :]).astype(np.float64)
    angle = 2 * np.pi * (local[:, None] * local[None, :] % MLOC) / MLOC
    cos, sin = same * np.cos(angle), same * np.sin(angle)
    middle = np.block([[cos, -sin], [sin, cos]])
    angle = 2 * np.pi * (freq[:, None] * local[None, :]) / PERIOD
    turn = np.stack([np.cos(angle), np.sin(angle)]).astype(np.float32)
    return [*(table.astype(np.float32) for table in (first, middle, last)), turn]


def parts_of(x):
    high = x.astype(jnp.bfloat16)
    return high, (x - high.astype(jnp.float32)).astype(jnp.bfloat16)


def mm(a, b):
    return jnp.dot(a, b, preferred_element_type=jnp.float32)


def table_times(table, x):
    high, low = table
    xh, xl = parts_of(x)
    return mm(high, xh) + (mm(high, xl) + mm(low, xh))


def times_table(x, table):
    high, low = table
    xh, xl = parts_of(x)
    return mm(xh, high) + (mm(xl, high) + mm(xh, low))


def turned(real, imag, cos, sin):
    return real * cos + imag * sin, imag * cos - real * sin


def both(left, right):
    return jnp.concatenate([left, right], axis=1)


def forward(rows, first, middle, cos, sin):
    y = table_times(first, rows)
    return times_table(both(*turned(y[:ROWS], y[ROWS:], cos, sin)), middle)


def conjugate(z):
    return both(z[:, :LANES], -z[:, LANES:])


def product(a, b):
    ar, ai, br, bi = a[:, :LANES], a[:, LANES:], b[:, :LANES], b[:, LANES:]
    return both(ar * br + ai * bi, ai * br - ar * bi)


def inverse(z, middle, last, cos, sin):
    v = times_table(z, middle)
    return table_times(last, jnp.concatenate(turned(v[:, :LANES], v[:, LANES:], cos, sin), 0))


def blocks_swapped(t):
    cut = [[t[32 * i : 32 * i + 32, 32 * j : 32 * j + 32] for j in range(4)] for i in range(4)]
    return [jnp.concatenate([cut[i][j] for i in range(4)], axis=1) for j in range(4)]


def to_owner(block, out):
    t = jnp.concatenate([block(zl) for zl in range(DEPTH)], 0).T
    for zl, rows in enumerate(blocks_swapped(t)):
        out[:, zl, :] = rows


def to_energies(got, store):
    rows = jnp.concatenate([got[:, zl, :] for zl in range(DEPTH)], 0)
    t = jnp.concatenate(blocks_swapped(rows), 0).T
    for zl in range(DEPTH):
        store(zl, t[MLOC * zl : MLOC * zl + MLOC])


def permuted(src, order, d):
    at = jnp.broadcast_to(order[d], (8, LANES))
    lane, where = at % LANES, at // LANES
    total = jnp.take_along_axis(src[:, :LANES], lane, axis=1)
    for s in range(1, LINE):
        moved = jnp.take_along_axis(src[:, s * LANES : (s + 1) * LANES], lane, axis=1)
        total = jnp.where(where == s, moved, total)
    return total


def kernel(
    lesser, greater, partner, *refs,
):
    tables_in, refs = refs[:4], refs[4:]
    lesser_out, greater_out = refs[:2]
    tables_here, halves, refs = refs[2:6], refs[6:9], refs[9:]
    (
        order, z1, swapped, z2, lesser_here, send_a, mid_a, deep_a, own_a, freq_a, send_b, own_b,
        back_q, got_q, wide_q, z2_back, unswapped, freq_p, back_p, mid_p, send_p, got_p, lesser_done,
        table_sem, sems, line_send, plane_send, few_send, here,
    ) = refs
    energy, zh = lax.axis_index("energy"), lax.axis_index("elem")
    w, zl = energy // 8 * 2 + energy % 2, energy // 2 % DEPTH
    z = zh * DEPTH + zl
    parts = (0, 1)

    def device(plane, low, high):
        return {"energy": plane // 2 * 8 + low * 2 + plane % 2, "elem": high}

    def line_peer(i):
        other = (z + LINE + (LINE // 2 - (i + 1) // 2) * (1 - 2 * (i % 2))) % LINE
        return other % DEPTH, other // DEPTH

    def flips(value, *weights):
        return [weight * (1 - 2 * (value // weight % 2)) for weight in weights]

    def flipped(value, steps, k):
        return value + sum(step for bit, step in enumerate(steps) if k >> bit & 1)

    plane_flips, w_flips = flips(energy, 1, 8, 16, 32, 64), flips(w, 1, 2, 4, 8, 16)
    depth_flips, zl_flips, zh_flips = flips(energy, 2, 4), flips(zl, 1, 2), flips(zh, 1, 2)
    plane_peers = [
        (flipped(w, w_flips, k), {"energy": flipped(energy, plane_flips, k), "elem": zh})
        for k in PLANE_STEPS
    ]
    line_peers = [
        (
            flipped(zl, zl_flips, k % 4),
            flipped(zh, zh_flips, k // 4),
            {"energy": flipped(energy, depth_flips, k % 4), "elem": flipped(zh, zh_flips, k // 4)},
        )
        for k in LINE_STEPS
    ]

    def meet_zl(low):
        return (low + 2) % DEPTH

    def meet_zh(low, h):
        return (h + (low + 2) // DEPTH) % GROUPS

    def met_quarter(low, high):
        return (high + GROUPS - (3 - low) // 2) % GROUPS

    barrier = pltpu.get_barrier_semaphore()

    ring = [{"energy": flipped(energy, plane_flips, k), "elem": zh} for k in range(1, 8)]
    near = [{"energy": flipped(energy, plane_flips, k), "elem": zh} for k in (8, 16, 24)]
    near += [{"energy": flipped(energy, depth_flips, k), "elem": zh} for k in (1, 3)]
    near += [
        {"energy": flipped(energy, depth_flips, 2), "elem": flipped(zh, zh_flips, k)}
        for k in (2, 1, 3, 0)
    ]
    for where in near[::-1] + ring:
        pl.semaphore_signal(barrier, inc=1, device_id=where, device_id_type=MESH)
    table_copies = [
        pltpu.make_async_copy(src, dst, table_sem.at[i])
        for i, (src, dst) in enumerate(zip(tables_in, tables_here))
    ]
    for copy in table_copies:
        copy.start()
    lesser_copy = pltpu.make_async_copy(lesser, lesser_here, table_sem.at[4])
    lesser_copy.start()
    lesser_copy.wait()
    for part in parts:
        to_owner(lambda low: lesser_here[part, :, low * LANES : (low + 1) * LANES], send_a.at[part])
    pl.semaphore_wait(barrier, len(near) + len(ring))

    def remote(src, dst, send, recv, where):
        return pltpu.make_async_remote_copy(
            src_ref=src, dst_ref=dst, send_sem=send, recv_sem=recv,
            device_id=where, device_id_type=MESH,
        )

    def arrived(whole, sem):
        pltpu.make_async_copy(whole, whole, sem).wait()

    def quarter(ref, part, h):
        return ref.at[part, pl.ds(pl.multiple_of(h * 8, 8), 8), :]

    def lanes(ref, start, size):
        return ref.at[..., pl.ds(pl.multiple_of(start, LANES), size)]

    started = []

    def send(phase, i, src, dst, recv, where):
        copy = remote(src, dst, few_send.at[phase, i], recv, where)
        copy.start()
        started.append(copy)

    def meet(phase, src, dst, recv):
        for i in range(GROUPS):
            h = (zh + 1 + i) % GROUPS
            send(phase, i, src(h), dst, recv, device(w, meet_zl(zl), meet_zh(zl, h)))

    def depths(phase, src, dst, recv):
        for i in range(DEPTH - 1):
            low = (zl + 1 + i) % DEPTH
            send(phase, i, src(low), dst, recv, device(w, low, zh))
        pltpu.make_async_copy(src(zl), dst, recv).start()

    def line(phase, src, dst, recv, make=None):
        if make is None:
            for low, high, where in line_peers:
                remote(src(low, high), dst, line_send.at[phase], recv, where).start()
        else:

            def start(i, c):
                low, high = line_peer(i)
                make(low, high)
                remote(
                    src(low, high), dst, line_send.at[phase], recv, device(w, low, high)
                ).start()
                return c

            lax.fori_loop(0, LINE - 1, start, 0, unroll=3)
            make(zl, zh)
        pltpu.make_async_copy(src(zl, zh), dst, recv).start()

    def line_done(phase):
        arrived(swapped.at[0, :, pl.ds(0, (LINE - 1) * LANES)], line_send.at[phase])

    def plane(phase, src, dst, recv):
        for other, where in plane_peers:
            remote(src(other), dst(w), plane_send.at[phase], recv, where).start()
        pltpu.make_async_copy(src(w), dst(w), recv).start()

    def plane_done(phase, blocks):
        arrived(blocks, plane_send.at[phase])

    def both_parts(ref):
        return lambda other: ref.at[:, other]

    def one_part(ref, part):
        return lambda other: ref.at[part, other]

    def make_tile(src, dst):
        def make(low, high):
            d = high * DEPTH + low
            dst[:, pl.ds(pl.multiple_of(d * LANES, LANES), LANES)] = permuted(src, flat, d)

        return make

    for i in range(GROUPS):
        h = (zh + 1 + i) % GROUPS
        send(0, i, partner, order.at[zh], sems.at[0], device(w, meet_zl(zl), h))
    for part in parts:
        meet(1 + part, lambda h: quarter(greater, part, h), lanes(z1.at[part], zh * 512, 512), sems.at[1 + part])
    for where in ring:
        pl.semaphore_signal(here, inc=1, device_id=where, device_id_type=MESH)
    pl.semaphore_wait(here, len(ring))
    plane(0, both_parts(send_a), both_parts(mid_a), sems.at[6])
    for copy in table_copies:
        copy.wait()
    for table, half in zip(tables_here, halves):
        half[0], half[1] = parts_of(table[...])
    first, middle, last = [lambda half=half: (half[0], half[1]) for half in halves]
    turn = tables_here[3]
    arrived(order, sems.at[0])
    flat = order.reshape(LINE, 1, LANES)

    def swapped_src(part):
        return lambda low, high: lanes(swapped.at[part], (high * DEPTH + low) * LANES, LANES)

    def z2_dst(part):
        return z2.at[part, meet_zl(zl), met_quarter(zl, zh)]

    for part in parts:
        arrived(z1.at[part], sems.at[1 + part])
        line(part, swapped_src(part), z2_dst(part), sems.at[4 + part], make_tile(z1.at[part], swapped.at[part]))
    arrived(mid_a, sems.at[6])
    for low in range(DEPTH):
        for part in parts:
            deep_a[low, part] = mid_a[part, :, low, :]
    depths(3, lambda low: deep_a.at[low], own_a.at[:, zl], sems.at[3])
    for part in parts:
        arrived(z2.at[part], sems.at[4 + part])
        to_owner(lambda low: z2[part, low].reshape(MLOC, LANES), send_b.at[part])
        plane(1 + part, one_part(send_b, part), one_part(own_b, part), sems.at[7 + part])
    arrived(own_a, sems.at[3])
    freq_a[...] = forward(own_a[...].reshape(ROWS, LANES), first(), middle(), turn[0], turn[1])
    for part in parts:
        arrived(own_b.at[part], sems.at[7 + part])
    rows_b = jnp.concatenate(
        [(own_b[part, :, low, :] if part == 0 else -own_b[part, :, low, :]) for part in parts for low in range(DEPTH)], 0
    )
    joint = product(freq_a[...], forward(rows_b, first(), middle(), turn[0], turn[1]))
    freq_p[...] = conjugate(joint)
    q = inverse(joint, middle(), last(), turn[0], turn[1])
    for part in parts:
        for low in range(DEPTH):
            back_q[part, :, low, :] = q[part * LANES + low * PLANE : part * LANES + (low + 1) * PLANE]
        plane(3 + part, one_part(back_q, part), one_part(got_q, part), sems.at[9 + part])
    p = inverse(freq_p[...], middle(), last(), turn[0], turn[1])
    for low in range(DEPTH):
        back_p[low, 0] = -p[low * PLANE : (low + 1) * PLANE]
        back_p[low, 1] = p[LANES + low * PLANE : LANES + (low + 1) * PLANE]
    depths(4, lambda low: back_p.at[low], mid_p.at[:, zl], sems.at[14])

    def wide_src(part):
        return lambda low, high: wide_q.at[part, meet_zl(low), met_quarter(low, high)]

    def back_dst(part):
        return lanes(z2_back.at[part], z * LANES, LANES)

    for part in parts:
        arrived(got_q.at[part], sems.at[9 + part])

        def keep_q(low, rows):
            wide_q[part, low] = rows.reshape(GROUPS, 8, LANES)

        to_energies(got_q.at[part], keep_q)
        line(2 + part, wide_src(part), back_dst(part), sems.at[12 + part])
    arrived(mid_p, sems.at[14])
    for part in parts:
        for low in range(DEPTH):
            send_p[part, :, low, :] = mid_p[part, low]
    plane(5, both_parts(send_p), both_parts(got_p), sems.at[11])
    for part in parts:
        arrived(z2_back.at[part], sems.at[12 + part])
        make = make_tile(z2_back.at[part], unswapped.at[part])
        for i in range(GROUPS):
            h = (zh + 1 + zl // 2 + i) % GROUPS
            for low in range(DEPTH):
                make(low, h)
            send(
                5 + part, i, lanes(unswapped.at[part], h * 512, 512),
                quarter(greater_out, part, met_quarter(zl, zh)), sems.at[15 + part],
                device(w, meet_zl(zl), h),
            )
    arrived(got_p, sems.at[11])
    for part in parts:

        def keep_p(low, rows):
            lesser_done[part, :, low * LANES : (low + 1) * LANES] = rows

        to_energies(got_p.at[part], keep_p)
    lesser_copy = pltpu.make_async_copy(lesser_done, lesser_out, table_sem.at[5])
    lesser_copy.start()
    for copy in started:
        copy.wait_send()
    plane_done(0, send_a.at[:, pl.ds(0, PLANE - 1)])
    plane_done(5, send_p.at[:, pl.ds(0, PLANE - 1)])
    for part in parts:
        line_done(part)
        line_done(2 + part)
        plane_done(1 + part, send_b.at[part, pl.ds(0, PLANE - 1)])
        plane_done(3 + part, back_q.at[part, pl.ds(0, PLANE - 1)])
    lesser_copy.wait()
    for part in parts:
        arrived(greater_out.at[part], sems.at[15 + part])


def per_device(lesser, greater, partner):
    f32 = jnp.float32
    field = jax.ShapeDtypeStruct((2, MLOC, 512), f32)
    owned = pltpu.VMEM((2, PLANE, DEPTH, LANES), f32)
    long = pltpu.VMEM((2, 8, 2048), f32)
    whole = pltpu.VMEM((2, MLOC, 512), f32)
    deep = pltpu.VMEM((DEPTH, 2, PLANE, LANES), f32)
    sorted_ = pltpu.VMEM((2, DEPTH, PLANE, LANES), f32)
    freq = pltpu.VMEM((ROWS, ROWS), f32)
    cut = pltpu.VMEM((2, DEPTH, GROUPS, 8, LANES), f32)
    anywhere = pl.BlockSpec(memory_space=pltpu.HBM)
    constants = [jnp.asarray(table) for table in tables()]
    return pl.pallas_call(
        kernel,
        out_shape=(field, field),
        in_specs=[anywhere] * 7,
        out_specs=(anywhere, anywhere),
        scratch_shapes=[
            *[pltpu.VMEM(table.shape, table.dtype) for table in constants],
            *[pltpu.VMEM((2, *table.shape), jnp.bfloat16) for table in constants[:3]],
            pltpu.VMEM((GROUPS, 4, 1, LANES), jnp.int32),
            long, long, cut, whole, owned, owned, deep, sorted_, freq, owned, owned,
            owned, owned, cut, long, long, freq, deep, sorted_, owned, owned, whole,
            pltpu.SemaphoreType.DMA((6,)),
            pltpu.SemaphoreType.DMA((17,)),
            pltpu.SemaphoreType.DMA((4,)),
            pltpu.SemaphoreType.DMA((6,)),
            pltpu.SemaphoreType.DMA((7, 4)),
            pltpu.SemaphoreType.REGULAR,
        ],
        compiler_params=pltpu.CompilerParams(
            collective_id=0, has_side_effects=True, vmem_limit_bytes=56 * 1024 * 1024
        ),
    )(lesser, greater, partner.reshape(4, 1, LANES), *constants)


def solution(mesh):
    placed = (P(None, "energy", "elem"), P(None, "energy", "elem"), P("elem"))
    return jax.shard_map(
        per_device,
        mesh=mesh,
        in_specs=placed,
        out_specs=(P(None, "energy", "elem"), P(None, "energy", "elem")),
        check_vma=False,
    )
```

```python
import jax
import jax.numpy as jnp
import numpy as np
from jax import lax
from jax.experimental import pallas as pl
from jax.experimental.pallas import tpu as pltpu
from jax.sharding import PartitionSpec as P

PLANE, DEPTH, GROUPS, MLOC = 32, 4, 4, 32
LINE = DEPTH * GROUPS
ROWS, LANES = 256, 128
PERIOD = 8192
MESH = pl.DeviceIdType.MESH
HOPS = (0, 1, 2, 1)
PLANE_STEPS = sorted(range(1, PLANE), key=lambda k: -HOPS[k >> 3] - HOPS[k >> 1 & 3])
LINE_STEPS = (8, 9, 10, 11, 7, 6, 14, 13, 5, 12, 4, 15, 3, 2, 1)


def tables():
    row = np.arange(ROWS)
    part, zl, plane = row // LANES, row // PLANE % DEPTH, row % PLANE
    index = plane // 2 * 8 + zl * 2 + plane % 2
    freq = np.arange(ROWS)
    angle = 2 * np.pi * (freq[:, None] * index[None, :] % ROWS) / ROWS
    cos, sin = np.cos(angle), np.sin(angle)
    first = np.concatenate(
        [np.where(part == 0, cos, sin), np.where(part == 0, -sin, cos)], 0
    )
    last = np.concatenate(
        [np.where(part == 0, sin, cos).T, np.where(part == 0, -cos, sin).T], 1
    )
    lane = np.arange(LANES)
    local, el = lane % MLOC, lane // MLOC
    same = (el[:, None] == el[None, :]).astype(np.float64)
    angle = 2 * np.pi * (local[:, None] * local[None, :] % MLOC) / MLOC
    cos, sin = same * np.cos(angle), same * np.sin(angle)
    middle = np.block([[cos, -sin], [sin, cos]])
    angle = 2 * np.pi * (freq[:, None] * local[None, :]) / PERIOD
    turn = np.stack([np.cos(angle), np.sin(angle)]).astype(np.float32)
    return [*(table.astype(np.float32) for table in (first, middle, last)), turn]


def parts_of(x):
    high = x.astype(jnp.bfloat16)
    return high, (x - high.astype(jnp.float32)).astype(jnp.bfloat16)


def mm(a, b):
    return jnp.dot(a, b, preferred_element_type=jnp.float32)


def table_times(table, x):
    high, low = table
    xh, xl = parts_of(x)
    return mm(high, xh) + (mm(high, xl) + mm(low, xh))


def times_table(x, table):
    high, low = table
    xh, xl = parts_of(x)
    return mm(xh, high) + (mm(xl, high) + mm(xh, low))


def turned(real, imag, cos, sin):
    return real * cos + imag * sin, imag * cos - real * sin


def both(left, right):
    return jnp.concatenate([left, right], axis=1)


def forward(rows, first, middle, cos, sin):
    y = table_times(first, rows)
    return times_table(both(*turned(y[:ROWS], y[ROWS:], cos, sin)), middle)


def conjugate(z):
    return both(z[:, :LANES], -z[:, LANES:])


def product(a, b):
    ar, ai, br, bi = a[:, :LANES], a[:, LANES:], b[:, :LANES], b[:, LANES:]
    return both(ar * br + ai * bi, ai * br - ar * bi)


def inverse(z, middle, last, cos, sin):
    v = times_table(z, middle)
    return table_times(last, jnp.concatenate(turned(v[:, :LANES], v[:, LANES:], cos, sin), 0))


def blocks_swapped(t):
    cut = [[t[32 * i : 32 * i + 32, 32 * j : 32 * j + 32] for j in range(4)] for i in range(4)]
    return [jnp.concatenate([cut[i][j] for i in range(4)], axis=1) for j in range(4)]


def to_owner(block, out):
    t = jnp.concatenate([block(zl) for zl in range(DEPTH)], 0).T
    for zl, rows in enumerate(blocks_swapped(t)):
        out[:, zl, :] = rows


def to_energies(got, store):
    rows = jnp.concatenate([got[:, zl, :] for zl in range(DEPTH)], 0)
    t = jnp.concatenate(blocks_swapped(rows), 0).T
    for zl in range(DEPTH):
        store(zl, t[MLOC * zl : MLOC * zl + MLOC])


def permuted(src, order, d):
    at = jnp.broadcast_to(order[d], (8, LANES))
    lane, where = at % LANES, at // LANES
    total = jnp.take_along_axis(src[:, :LANES], lane, axis=1)
    for s in range(1, LINE):
        moved = jnp.take_along_axis(src[:, s * LANES : (s + 1) * LANES], lane, axis=1)
        total = jnp.where(where == s, moved, total)
    return total


def kernel(
    lesser, greater, partner, *refs,
):
    tables_in, refs = refs[:4], refs[4:]
    lesser_out, greater_out = refs[:2]
    tables_here, halves, refs = refs[2:6], refs[6:9], refs[9:]
    (
        order, z1, swapped, z2, lesser_here, send_a, mid_a, deep_a, own_a, freq_a, send_b, own_b,
        back_q, got_q, wide_q, z2_back, unswapped, freq_p, back_p, mid_p, send_p, got_p, lesser_done,
        table_sem, sems, line_send, plane_send, few_send, here,
    ) = refs
    energy, zh = lax.axis_index("energy"), lax.axis_index("elem")
    w, zl = energy // 8 * 2 + energy % 2, energy // 2 % DEPTH
    z = zh * DEPTH + zl
    parts = (0, 1)

    def device(plane, low, high):
        return {"energy": plane // 2 * 8 + low * 2 + plane % 2, "elem": high}

    def line_peer(i):
        other = (z + LINE + (LINE // 2 - (i + 1) // 2) * (1 - 2 * (i % 2))) % LINE
        return other % DEPTH, other // DEPTH

    def flips(value, *weights):
        return [weight * (1 - 2 * (value // weight % 2)) for weight in weights]

    def flipped(value, steps, k):
        return value + sum(step for bit, step in enumerate(steps) if k >> bit & 1)

    plane_flips, w_flips = flips(energy, 1, 8, 16, 32, 64), flips(w, 1, 2, 4, 8, 16)
    depth_flips, zl_flips, zh_flips = flips(energy, 2, 4), flips(zl, 1, 2), flips(zh, 1, 2)
    plane_peers = [
        (flipped(w, w_flips, k), {"energy": flipped(energy, plane_flips, k), "elem": zh})
        for k in PLANE_STEPS
    ]
    line_peers = [
        (
            flipped(zl, zl_flips, k % 4),
            flipped(zh, zh_flips, k // 4),
            {"energy": flipped(energy, depth_flips, k % 4), "elem": flipped(zh, zh_flips, k // 4)},
        )
        for k in LINE_STEPS
    ]

    def meet_zl(low):
        return (low + 2) % DEPTH

    def meet_zh(low, h):
        return (h + (low + 2) // DEPTH) % GROUPS

    def met_quarter(low, high):
        return (high + GROUPS - (3 - low) // 2) % GROUPS

    barrier = pltpu.get_barrier_semaphore()

    ring = [{"energy": flipped(energy, plane_flips, k), "elem": zh} for k in range(1, 8)]
    near = [{"energy": flipped(energy, plane_flips, k), "elem": zh} for k in (8, 16, 24)]
    near += [{"energy": flipped(energy, depth_flips, k), "elem": zh} for k in (1, 3)]
    near += [
        {"energy": flipped(energy, depth_flips, 2), "elem": flipped(zh, zh_flips, k)}
        for k in (2, 1, 3, 0)
    ]
    for where in near[::-1] + ring:
        pl.semaphore_signal(barrier, inc=1, device_id=where, device_id_type=MESH)
    table_copies = [
        pltpu.make_async_copy(src, dst, table_sem.at[i])
        for i, (src, dst) in enumerate(zip(tables_in, tables_here))
    ]
    for copy in table_copies:
        copy.start()
    lesser_copy = pltpu.make_async_copy(lesser, lesser_here, table_sem.at[4])
    lesser_copy.start()
    lesser_copy.wait()
    for part in parts:
        to_owner(lambda low: lesser_here[part, :, low * LANES : (low + 1) * LANES], send_a.at[part])
    pl.semaphore_wait(barrier, len(near) + len(ring))

    def remote(src, dst, send, recv, where):
        return pltpu.make_async_remote_copy(
            src_ref=src, dst_ref=dst, send_sem=send, recv_sem=recv,
            device_id=where, device_id_type=MESH,
        )

    def arrived(whole, sem):
        pltpu.make_async_copy(whole, whole, sem).wait()

    def quarter(ref, part, h):
        return ref.at[part, pl.ds(pl.multiple_of(h * 8, 8), 8), :]

    def lanes(ref, start, size):
        return ref.at[..., pl.ds(pl.multiple_of(start, LANES), size)]

    started = []

    def send(phase, i, src, dst, recv, where):
        copy = remote(src, dst, few_send.at[phase, i], recv, where)
        copy.start()
        started.append(copy)

    def meet(phase, src, dst, recv):
        for i in range(GROUPS):
            h = (zh + 1 + i) % GROUPS
            send(phase, i, src(h), dst, recv, device(w, meet_zl(zl), meet_zh(zl, h)))

    def depths(phase, src, dst, recv):
        for i in range(DEPTH - 1):
            low = (zl + 1 + i) % DEPTH
            send(phase, i, src(low), dst, recv, device(w, low, zh))
        pltpu.make_async_copy(src(zl), dst, recv).start()

    def line(phase, src, dst, recv, make=None):
        if make is None:
            for low, high, where in line_peers:
                remote(src(low, high), dst, line_send.at[phase], recv, where).start()
        else:

            def start(i, c):
                low, high = line_peer(i)
                make(low, high)
                remote(
                    src(low, high), dst, line_send.at[phase], recv, device(w, low, high)
                ).start()
                return c

            lax.fori_loop(0, LINE - 1, start, 0, unroll=3)
            make(zl, zh)
        pltpu.make_async_copy(src(zl, zh), dst, recv).start()

    def line_done(phase):
        arrived(swapped.at[0, :, pl.ds(0, (LINE - 1) * LANES)], line_send.at[phase])

    def plane(phase, src, dst, recv):
        for other, where in plane_peers:
            remote(src(other), dst(w), plane_send.at[phase], recv, where).start()
        pltpu.make_async_copy(src(w), dst(w), recv).start()

    def plane_done(phase, blocks):
        arrived(blocks, plane_send.at[phase])

    def both_parts(ref):
        return lambda other: ref.at[:, other]

    def one_part(ref, part):
        return lambda other: ref.at[part, other]

    def make_tile(src, dst):
        def make(low, high):
            d = high * DEPTH + low
            dst[:, pl.ds(pl.multiple_of(d * LANES, LANES), LANES)] = permuted(src, flat, d)

        return make

    for i in range(GROUPS):
        h = (zh + 1 + i) % GROUPS
        send(0, i, partner, order.at[zh], sems.at[0], device(w, meet_zl(zl), h))
    for part in parts:
        meet(1 + part, lambda h: quarter(greater, part, h), lanes(z1.at[part], zh * 512, 512), sems.at[1 + part])
    for where in ring:
        pl.semaphore_signal(here, inc=1, device_id=where, device_id_type=MESH)
    pl.semaphore_wait(here, len(ring))
    plane(0, both_parts(send_a), both_parts(mid_a), sems.at[6])
    for copy in table_copies:
        copy.wait()
    for table, half in zip(tables_here, halves):
        half[0], half[1] = parts_of(table[...])
    first, middle, last = [lambda half=half: (half[0], half[1]) for half in halves]
    turn = tables_here[3]
    arrived(order, sems.at[0])
    flat = order.reshape(LINE, 1, LANES)

    def swapped_src(part):
        return lambda low, high: lanes(swapped.at[part], (high * DEPTH + low) * LANES, LANES)

    def z2_dst(part):
        return z2.at[part, meet_zl(zl), met_quarter(zl, zh)]

    for part in parts:
        arrived(z1.at[part], sems.at[1 + part])
        line(part, swapped_src(part), z2_dst(part), sems.at[4 + part], make_tile(z1.at[part], swapped.at[part]))
    arrived(mid_a, sems.at[6])
    for low in range(DEPTH):
        for part in parts:
            deep_a[low, part] = mid_a[part, :, low, :]
    depths(3, lambda low: deep_a.at[low], own_a.at[:, zl], sems.at[3])
    for part in parts:
        arrived(z2.at[part], sems.at[4 + part])
        to_owner(lambda low: z2[part, low].reshape(MLOC, LANES), send_b.at[part])
        plane(1 + part, one_part(send_b, part), one_part(own_b, part), sems.at[7 + part])
    arrived(own_a, sems.at[3])
    freq_a[...] = forward(own_a[...].reshape(ROWS, LANES), first(), middle(), turn[0], turn[1])
    for part in parts:
        arrived(own_b.at[part], sems.at[7 + part])
    rows_b = jnp.concatenate(
        [(own_b[part, :, low, :] if part == 0 else -own_b[part, :, low, :]) for part in parts for low in range(DEPTH)], 0
    )
    joint = product(freq_a[...], forward(rows_b, first(), middle(), turn[0], turn[1]))
    freq_p[...] = conjugate(joint)
    q = inverse(joint, middle(), last(), turn[0], turn[1])
    for part in parts:
        for low in range(DEPTH):
            back_q[part, :, low, :] = q[part * LANES + low * PLANE : part * LANES + (low + 1) * PLANE]
        plane(3 + part, one_part(back_q, part), one_part(got_q, part), sems.at[9 + part])
    p = inverse(freq_p[...], middle(), last(), turn[0], turn[1])
    for low in range(DEPTH):
        back_p[low, 0] = -p[low * PLANE : (low + 1) * PLANE]
        back_p[low, 1] = p[LANES + low * PLANE : LANES + (low + 1) * PLANE]
    depths(4, lambda low: back_p.at[low], mid_p.at[:, zl], sems.at[14])

    def wide_src(part):
        return lambda low, high: wide_q.at[part, meet_zl(low), met_quarter(low, high)]

    def back_dst(part):
        return lanes(z2_back.at[part], z * LANES, LANES)

    for part in parts:
        arrived(got_q.at[part], sems.at[9 + part])

        def keep_q(low, rows):
            wide_q[part, low] = rows.reshape(GROUPS, 8, LANES)

        to_energies(got_q.at[part], keep_q)
        line(2 + part, wide_src(part), back_dst(part), sems.at[12 + part])
    arrived(mid_p, sems.at[14])
    for part in parts:
        for low in range(DEPTH):
            send_p[part, :, low, :] = mid_p[part, low]
    plane(5, both_parts(send_p), both_parts(got_p), sems.at[11])

    def leave(part, h):
        make = make_tile(z2_back.at[part], unswapped.at[part])
        for low in range(DEPTH):
            make(low, h)
        send(
            5 + part, h, lanes(unswapped.at[part], h * 512, 512),
            quarter(greater_out, part, met_quarter(zl, zh)), sems.at[15 + part],
            device(w, meet_zl(zl), h),
        )

    for part in parts:
        arrived(z2_back.at[part], sems.at[12 + part])
        for h in (0, 1):
            leave(part, h)
    for part in parts:
        for h in (2, 3):
            leave(part, h)
    arrived(got_p, sems.at[11])
    for part in parts:

        def keep_p(low, rows):
            lesser_done[part, :, low * LANES : (low + 1) * LANES] = rows

        to_energies(got_p.at[part], keep_p)
    lesser_copy = pltpu.make_async_copy(lesser_done, lesser_out, table_sem.at[5])
    lesser_copy.start()
    for copy in started:
        copy.wait_send()
    plane_done(0, send_a.at[:, pl.ds(0, PLANE - 1)])
    plane_done(5, send_p.at[:, pl.ds(0, PLANE - 1)])
    for part in parts:
        line_done(part)
        line_done(2 + part)
        plane_done(1 + part, send_b.at[part, pl.ds(0, PLANE - 1)])
        plane_done(3 + part, back_q.at[part, pl.ds(0, PLANE - 1)])
    lesser_copy.wait()
    for part in parts:
        arrived(greater_out.at[part], sems.at[15 + part])


def per_device(lesser, greater, partner):
    f32 = jnp.float32
    field = jax.ShapeDtypeStruct((2, MLOC, 512), f32)
    owned = pltpu.VMEM((2, PLANE, DEPTH, LANES), f32)
    long = pltpu.VMEM((2, 8, 2048), f32)
    whole = pltpu.VMEM((2, MLOC, 512), f32)
    deep = pltpu.VMEM((DEPTH, 2, PLANE, LANES), f32)
    sorted_ = pltpu.VMEM((2, DEPTH, PLANE, LANES), f32)
    freq = pltpu.VMEM((ROWS, ROWS), f32)
    cut = pltpu.VMEM((2, DEPTH, GROUPS, 8, LANES), f32)
    anywhere = pl.BlockSpec(memory_space=pltpu.HBM)
    constants = [jnp.asarray(table) for table in tables()]
    lesser_polar, greater_polar = pl.pallas_call(
        kernel,
        out_shape=(field, field),
        in_specs=[anywhere] * 7,
        out_specs=(anywhere, anywhere),
        scratch_shapes=[
            *[pltpu.VMEM(table.shape, table.dtype) for table in constants],
            *[pltpu.VMEM((2, *table.shape), jnp.bfloat16) for table in constants[:3]],
            pltpu.VMEM((GROUPS, 4, 1, LANES), jnp.int32),
            long, long, cut, whole, owned, owned, deep, sorted_, freq, owned, owned,
            owned, owned, cut, long, long, freq, deep, sorted_, owned, owned, whole,
            pltpu.SemaphoreType.DMA((6,)),
            pltpu.SemaphoreType.DMA((17,)),
            pltpu.SemaphoreType.DMA((4,)),
            pltpu.SemaphoreType.DMA((6,)),
            pltpu.SemaphoreType.DMA((7, 4)),
            pltpu.SemaphoreType.REGULAR,
        ],
        compiler_params=pltpu.CompilerParams(
            collective_id=0, has_side_effects=True, vmem_limit_bytes=56 * 1024 * 1024
        ),
    )(lesser, greater, partner.reshape(4, 1, LANES), *constants)
    scale = 1.0 / (64 * PERIOD)
    return lesser_polar * scale, greater_polar * scale


def solution(mesh):
    placed = (P(None, "energy", "elem"), P(None, "energy", "elem"), P("elem"))
    return jax.shard_map(
        per_device,
        mesh=mesh,
        in_specs=placed,
        out_specs=(P(None, "energy", "elem"), P(None, "energy", "elem")),
        check_vma=False,
    )
```

```python
import jax
import jax.numpy as jnp
import numpy as np
from jax import lax
from jax.experimental import pallas as pl
from jax.experimental.pallas import tpu as pltpu
from jax.sharding import PartitionSpec as P

PLANE, DEPTH, GROUPS, MLOC = 32, 4, 4, 32
LINE = DEPTH * GROUPS
ROWS, LANES = 256, 128
PERIOD = 8192
MESH = pl.DeviceIdType.MESH
HOPS = (0, 1, 2, 1)
PLANE_STEPS = sorted(range(1, PLANE), key=lambda k: -HOPS[k >> 3] - HOPS[k >> 1 & 3])
LINE_STEPS = (8, 9, 10, 11, 7, 6, 14, 13, 5, 12, 4, 15, 3, 2, 1)


def tables():
    row = np.arange(ROWS)
    part, zl, plane = row // LANES, row // PLANE % DEPTH, row % PLANE
    index = plane // 2 * 8 + zl * 2 + plane % 2
    freq = np.arange(ROWS)
    angle = 2 * np.pi * (freq[:, None] * index[None, :] % ROWS) / ROWS
    cos, sin = np.cos(angle), np.sin(angle)
    first = np.concatenate(
        [np.where(part == 0, cos, sin), np.where(part == 0, -sin, cos)], 0
    )
    last = np.concatenate(
        [np.where(part == 0, sin, cos).T, np.where(part == 0, -cos, sin).T], 1
    )
    lane = np.arange(LANES)
    local, el = lane % MLOC, lane // MLOC
    same = (el[:, None] == el[None, :]).astype(np.float64)
    angle = 2 * np.pi * (local[:, None] * local[None, :] % MLOC) / MLOC
    cos, sin = same * np.cos(angle), same * np.sin(angle)
    middle = np.block([[cos, -sin], [sin, cos]])
    angle = 2 * np.pi * (freq[:, None] * local[None, :]) / PERIOD
    turn = np.stack([np.cos(angle), np.sin(angle)]).astype(np.float32)
    return [*(table.astype(np.float32) for table in (first, middle, last)), turn]


def parts_of(x):
    high = x.astype(jnp.bfloat16)
    return high, (x - high.astype(jnp.float32)).astype(jnp.bfloat16)


def mm(a, b):
    return jnp.dot(a, b, preferred_element_type=jnp.float32)


def table_times(table, x):
    high, low = table
    xh, xl = parts_of(x)
    return mm(high, xh) + (mm(high, xl) + mm(low, xh))


def times_table(x, table):
    high, low = table
    xh, xl = parts_of(x)
    return mm(xh, high) + (mm(xl, high) + mm(xh, low))


def turned(real, imag, cos, sin):
    return real * cos + imag * sin, imag * cos - real * sin


def both(left, right):
    return jnp.concatenate([left, right], axis=1)


def forward(rows, first, middle, cos, sin):
    y = table_times(first, rows)
    return times_table(both(*turned(y[:ROWS], y[ROWS:], cos, sin)), middle)


def conjugate(z):
    return both(z[:, :LANES], -z[:, LANES:])


def product(a, b):
    ar, ai, br, bi = a[:, :LANES], a[:, LANES:], b[:, :LANES], b[:, LANES:]
    return both(ar * br + ai * bi, ai * br - ar * bi)


def inverse(z, middle, last, cos, sin):
    v = times_table(z, middle)
    return table_times(last, jnp.concatenate(turned(v[:, :LANES], v[:, LANES:], cos, sin), 0))


def blocks_swapped(t):
    cut = [[t[32 * i : 32 * i + 32, 32 * j : 32 * j + 32] for j in range(4)] for i in range(4)]
    return [jnp.concatenate([cut[i][j] for i in range(4)], axis=1) for j in range(4)]


def to_owner(block, out):
    t = jnp.concatenate([block(zl) for zl in range(DEPTH)], 0).T
    for zl, rows in enumerate(blocks_swapped(t)):
        out[:, zl, :] = rows


def to_energies(got, store):
    rows = jnp.concatenate([got[:, zl, :] for zl in range(DEPTH)], 0)
    t = jnp.concatenate(blocks_swapped(rows), 0).T
    for zl in range(DEPTH):
        store(zl, t[MLOC * zl : MLOC * zl + MLOC])


def permuted(src, order, d):
    at = jnp.broadcast_to(order[d], (8, LANES))
    lane, where = at % LANES, at // LANES
    total = jnp.take_along_axis(src[:, :LANES], lane, axis=1)
    for s in range(1, LINE):
        moved = jnp.take_along_axis(src[:, s * LANES : (s + 1) * LANES], lane, axis=1)
        total = jnp.where(where == s, moved, total)
    return total


def kernel(
    lesser, greater, partner, *refs,
):
    tables_in, refs = refs[:4], refs[4:]
    lesser_out, greater_out = refs[:2]
    tables_here, halves, refs = refs[2:6], refs[6:9], refs[9:]
    (
        order, z1, swapped, z2, lesser_here, send_a, mid_a, deep_a, own_a, freq_a, send_b, own_b,
        back_q, got_q, wide_q, z2_back, unswapped, freq_p, back_p, mid_p, send_p, got_p, lesser_done,
        table_sem, sems, line_send, plane_send, few_send, here,
    ) = refs
    energy, zh = lax.axis_index("energy"), lax.axis_index("elem")
    w, zl = energy // 8 * 2 + energy % 2, energy // 2 % DEPTH
    z = zh * DEPTH + zl
    parts = (0, 1)

    def device(plane, low, high):
        return {"energy": plane // 2 * 8 + low * 2 + plane % 2, "elem": high}

    def line_peer(i):
        other = (z + LINE + (LINE // 2 - (i + 1) // 2) * (1 - 2 * (i % 2))) % LINE
        return other % DEPTH, other // DEPTH

    def flips(value, *weights):
        return [weight * (1 - 2 * (value // weight % 2)) for weight in weights]

    def flipped(value, steps, k):
        return value + sum(step for bit, step in enumerate(steps) if k >> bit & 1)

    plane_flips, w_flips = flips(energy, 1, 8, 16, 32, 64), flips(w, 1, 2, 4, 8, 16)
    depth_flips, zl_flips, zh_flips = flips(energy, 2, 4), flips(zl, 1, 2), flips(zh, 1, 2)
    plane_peers = [
        (flipped(w, w_flips, k), {"energy": flipped(energy, plane_flips, k), "elem": zh})
        for k in PLANE_STEPS
    ]
    line_peers = [
        (
            flipped(zl, zl_flips, k % 4),
            flipped(zh, zh_flips, k // 4),
            {"energy": flipped(energy, depth_flips, k % 4), "elem": flipped(zh, zh_flips, k // 4)},
        )
        for k in LINE_STEPS
    ]

    def meet_zl(low):
        return (low + 2) % DEPTH

    def meet_zh(low, h):
        return (h + (low + 2) // DEPTH) % GROUPS

    def met_quarter(low, high):
        return (high + GROUPS - (3 - low) // 2) % GROUPS

    barrier = pltpu.get_barrier_semaphore()

    ring = [{"energy": flipped(energy, plane_flips, k), "elem": zh} for k in range(1, 8)]
    near = [{"energy": flipped(energy, plane_flips, k), "elem": zh} for k in (8, 16, 24)]
    near += [{"energy": flipped(energy, depth_flips, k), "elem": zh} for k in (1, 3)]
    near += [
        {"energy": flipped(energy, depth_flips, 2), "elem": flipped(zh, zh_flips, k)}
        for k in (2, 1, 3, 0)
    ]
    for where in near[::-1] + ring:
        pl.semaphore_signal(barrier, inc=1, device_id=where, device_id_type=MESH)
    table_copies = [
        pltpu.make_async_copy(src, dst, table_sem.at[i])
        for i, (src, dst) in enumerate(zip(tables_in, tables_here))
    ]
    for copy in table_copies:
        copy.start()
    lesser_copy = pltpu.make_async_copy(lesser, lesser_here, table_sem.at[4])
    lesser_copy.start()
    lesser_copy.wait()
    for part in parts:
        to_owner(lambda low: lesser_here[part, :, low * LANES : (low + 1) * LANES], send_a.at[part])
    pl.semaphore_wait(barrier, len(near) + len(ring))

    def remote(src, dst, send, recv, where):
        return pltpu.make_async_remote_copy(
            src_ref=src, dst_ref=dst, send_sem=send, recv_sem=recv,
            device_id=where, device_id_type=MESH,
        )

    def arrived(whole, sem):
        pltpu.make_async_copy(whole, whole, sem).wait()

    def quarter(ref, part, h):
        return ref.at[part, pl.ds(pl.multiple_of(h * 8, 8), 8), :]

    def lanes(ref, start, size):
        return ref.at[..., pl.ds(pl.multiple_of(start, LANES), size)]

    started = []

    def send(phase, i, src, dst, recv, where):
        copy = remote(src, dst, few_send.at[phase, i], recv, where)
        copy.start()
        started.append(copy)

    def meet(phase, src, dst, recv):
        for i in range(GROUPS):
            h = (zh + 1 + i) % GROUPS
            send(phase, i, src(h), dst, recv, device(w, meet_zl(zl), meet_zh(zl, h)))

    def depths(phase, src, dst, recv):
        for i in range(DEPTH - 1):
            low = (zl + 1 + i) % DEPTH
            send(phase, i, src(low), dst, recv, device(w, low, zh))
        pltpu.make_async_copy(src(zl), dst, recv).start()

    def line(phase, src, dst, recv, make=None):
        if make is None:
            for low, high, where in line_peers:
                remote(src(low, high), dst, line_send.at[phase], recv, where).start()
        else:

            def start(i, c):
                low, high = line_peer(i)
                make(low, high)
                remote(
                    src(low, high), dst, line_send.at[phase], recv, device(w, low, high)
                ).start()
                return c

            lax.fori_loop(0, LINE - 1, start, 0, unroll=3)
            make(zl, zh)
        pltpu.make_async_copy(src(zl, zh), dst, recv).start()

    def line_done(phase):
        arrived(swapped.at[0, :, pl.ds(0, (LINE - 1) * LANES)], line_send.at[phase])

    def plane(phase, src, dst, recv):
        for other, where in plane_peers:
            remote(src(other), dst(w), plane_send.at[phase], recv, where).start()
        pltpu.make_async_copy(src(w), dst(w), recv).start()

    def plane_done(phase, blocks):
        arrived(blocks, plane_send.at[phase])

    def both_parts(ref):
        return lambda other: ref.at[:, other]

    def one_part(ref, part):
        return lambda other: ref.at[part, other]

    def make_tile(src, dst):
        def make(low, high):
            d = high * DEPTH + low
            dst[:, pl.ds(pl.multiple_of(d * LANES, LANES), LANES)] = permuted(src, flat, d)

        return make

    for i in range(GROUPS):
        h = (zh + 1 + i) % GROUPS
        send(0, i, partner, order.at[zh], sems.at[0], device(w, meet_zl(zl), h))
    for part in parts:
        meet(1 + part, lambda h: quarter(greater, part, h), lanes(z1.at[part], zh * 512, 512), sems.at[1 + part])
    for where in ring:
        pl.semaphore_signal(here, inc=1, device_id=where, device_id_type=MESH)
    pl.semaphore_wait(here, len(ring))
    plane(0, both_parts(send_a), both_parts(mid_a), sems.at[6])
    for copy in table_copies:
        copy.wait()
    for table, half in zip(tables_here, halves):
        half[0], half[1] = parts_of(table[...])
    first, middle, last = [lambda half=half: (half[0], half[1]) for half in halves]
    turn = tables_here[3]
    arrived(order, sems.at[0])
    flat = order.reshape(LINE, 1, LANES)

    def swapped_src(part):
        return lambda low, high: lanes(swapped.at[part], (high * DEPTH + low) * LANES, LANES)

    def z2_dst(part):
        return z2.at[part, meet_zl(zl), met_quarter(zl, zh)]

    for part in parts:
        arrived(z1.at[part], sems.at[1 + part])
        line(part, swapped_src(part), z2_dst(part), sems.at[4 + part], make_tile(z1.at[part], swapped.at[part]))
    arrived(mid_a, sems.at[6])
    for low in range(DEPTH):
        for part in parts:
            deep_a[low, part] = mid_a[part, :, low, :]
    depths(3, lambda low: deep_a.at[low], own_a.at[:, zl], sems.at[3])
    for part in parts:
        arrived(z2.at[part], sems.at[4 + part])
        to_owner(lambda low: z2[part, low].reshape(MLOC, LANES), send_b.at[part])
        plane(1 + part, one_part(send_b, part), one_part(own_b, part), sems.at[7 + part])
    arrived(own_a, sems.at[3])
    freq_a[...] = forward(own_a[...].reshape(ROWS, LANES), first(), middle(), turn[0], turn[1])
    for part in parts:
        arrived(own_b.at[part], sems.at[7 + part])
    rows_b = jnp.concatenate(
        [(own_b[part, :, low, :] if part == 0 else -own_b[part, :, low, :]) for part in parts for low in range(DEPTH)], 0
    )
    joint = product(freq_a[...], forward(rows_b, first(), middle(), turn[0], turn[1]))
    freq_p[...] = conjugate(joint)
    q = inverse(joint, middle(), last(), turn[0], turn[1])
    for part in parts:
        for low in range(DEPTH):
            back_q[part, :, low, :] = q[part * LANES + low * PLANE : part * LANES + (low + 1) * PLANE]
    plane(3, both_parts(back_q), both_parts(got_q), sems.at[9])
    p = inverse(freq_p[...], middle(), last(), turn[0], turn[1])
    for low in range(DEPTH):
        back_p[low, 0] = -p[low * PLANE : (low + 1) * PLANE]
        back_p[low, 1] = p[LANES + low * PLANE : LANES + (low + 1) * PLANE]
    depths(4, lambda low: back_p.at[low], mid_p.at[:, zl], sems.at[14])

    arrived(got_q, sems.at[9])
    for part in parts:

        def keep_q(low, rows):
            wide_q[part, low] = rows.reshape(GROUPS, 8, LANES)

        to_energies(got_q.at[part], keep_q)
    line(
        2, lambda low, high: wide_q.at[:, meet_zl(low), met_quarter(low, high)],
        lanes(z2_back, z * LANES, LANES), sems.at[12],
    )
    arrived(mid_p, sems.at[14])
    for part in parts:
        for low in range(DEPTH):
            send_p[part, :, low, :] = mid_p[part, low]
    plane(5, both_parts(send_p), both_parts(got_p), sems.at[11])

    arrived(z2_back, sems.at[12])
    for h in range(GROUPS):
        for part in parts:
            make = make_tile(z2_back.at[part], unswapped.at[part])
            for low in range(DEPTH):
                make(low, h)
        rows = pl.ds(pl.multiple_of(met_quarter(zl, zh) * 8, 8), 8)
        send(
            5, h, lanes(unswapped, h * 512, 512), greater_out.at[:, rows, :], sems.at[15],
            device(w, meet_zl(zl), h),
        )
    arrived(got_p, sems.at[11])
    for part in parts:

        def keep_p(low, rows):
            lesser_done[part, :, low * LANES : (low + 1) * LANES] = rows

        to_energies(got_p.at[part], keep_p)
    lesser_copy = pltpu.make_async_copy(lesser_done, lesser_out, table_sem.at[5])
    lesser_copy.start()
    for copy in started:
        copy.wait_send()
    plane_done(0, send_a.at[:, pl.ds(0, PLANE - 1)])
    plane_done(3, back_q.at[:, pl.ds(0, PLANE - 1)])
    arrived(swapped.at[:, :, pl.ds(0, (LINE - 1) * LANES)], line_send.at[2])
    plane_done(5, send_p.at[:, pl.ds(0, PLANE - 1)])
    for part in parts:
        line_done(part)
        plane_done(1 + part, send_b.at[part, pl.ds(0, PLANE - 1)])
    lesser_copy.wait()
    arrived(greater_out, sems.at[15])


def per_device(lesser, greater, partner):
    f32 = jnp.float32
    field = jax.ShapeDtypeStruct((2, MLOC, 512), f32)
    owned = pltpu.VMEM((2, PLANE, DEPTH, LANES), f32)
    long = pltpu.VMEM((2, 8, 2048), f32)
    whole = pltpu.VMEM((2, MLOC, 512), f32)
    deep = pltpu.VMEM((DEPTH, 2, PLANE, LANES), f32)
    sorted_ = pltpu.VMEM((2, DEPTH, PLANE, LANES), f32)
    freq = pltpu.VMEM((ROWS, ROWS), f32)
    cut = pltpu.VMEM((2, DEPTH, GROUPS, 8, LANES), f32)
    anywhere = pl.BlockSpec(memory_space=pltpu.HBM)
    constants = [jnp.asarray(table) for table in tables()]
    lesser_polar, greater_polar = pl.pallas_call(
        kernel,
        out_shape=(field, field),
        in_specs=[anywhere] * 7,
        out_specs=(anywhere, anywhere),
        scratch_shapes=[
            *[pltpu.VMEM(table.shape, table.dtype) for table in constants],
            *[pltpu.VMEM((2, *table.shape), jnp.bfloat16) for table in constants[:3]],
            pltpu.VMEM((GROUPS, 4, 1, LANES), jnp.int32),
            long, long, cut, whole, owned, owned, deep, sorted_, freq, owned, owned,
            owned, owned, cut, long, long, freq, deep, sorted_, owned, owned, whole,
            pltpu.SemaphoreType.DMA((6,)),
            pltpu.SemaphoreType.DMA((17,)),
            pltpu.SemaphoreType.DMA((4,)),
            pltpu.SemaphoreType.DMA((6,)),
            pltpu.SemaphoreType.DMA((7, 4)),
            pltpu.SemaphoreType.REGULAR,
        ],
        compiler_params=pltpu.CompilerParams(
            collective_id=0, has_side_effects=True, vmem_limit_bytes=56 * 1024 * 1024
        ),
    )(lesser, greater, partner.reshape(4, 1, LANES), *constants)
    scale = 1.0 / (64 * PERIOD)
    return lesser_polar * scale, greater_polar * scale


def solution(mesh):
    placed = (P(None, "energy", "elem"), P(None, "energy", "elem"), P("elem"))
    return jax.shard_map(
        per_device,
        mesh=mesh,
        in_specs=placed,
        out_specs=(P(None, "energy", "elem"), P(None, "energy", "elem")),
        check_vma=False,
    )
```
